32 devices in a mesh: gx: 4 (over y, core), gy: 8 (over z, x).
Axes of the slice: x: 2, y: 2, z: 4, core: 2. Of those that a mesh axis runs over, the one named last changes fastest.
Arguments:
- cell_state: float32 [16, 262144], P(None, ('gx', 'gy')), may hold values from -6 to 6
- geometry: float32 [7, 131072], P(None, ('gx', 'gy')), may hold values from -8 to 8, as said below
- surface_cell: int32 [131072], P(('gx', 'gy')), may hold values from 0 to 8191
- counts: int32 [32], P(('gx', 'gy')), may hold values from 32 to 4096, as said below
- wavenumbers: float32 [4], replicated, may hold values from 8 to 24
- target: float32 [4, 2, 2048], replicated, may hold values from -6 to 6
- direction_weight: float32 [2048], replicated, may hold values from 0.3 to 3
Outputs:
- far_field: float32 [4, 2, 2048], replicated
- objective: float32 [], replicated
- cell_adjoint: float32 [16, 262144], P(None, ('gx', 'gy'))
The draws below stay inside these ranges and needn't reach their ends.
Inputs may be any that keep to these rules, and one draw needn't show every extreme that they name: Every count is a multiple of 32; one device's count is 4096; all counts together make 32 * 1024. `geometry`: rows 3 to 5 are unit vectors; row 6 is positive.
All inputs are finite; a program needn't handle non-finite values.
Results may differ from the reference program's by a relative error of at most 0.022.
Values sent between devices are 32-bit elements; how exact they have to be, the bound alone decides.
No kernel may reach another device: no remote copies, remote signals or barrier semaphores. Data moves between devices by JAX's collectives and lax.ppermute only.
A program may use at most 128 MiB of HBM per device.

```python
import math
import jax
import jax.numpy as jnp
from jax import lax

F = 4
DIRS = 2048
ROWS_DEV = 4096
OWNERS = 32
CAP = 128
LIVE_OWN = 1024
LIVE_ALL = 32768
ROWS = 131072
CELLS_DEV = 8192
CELLS = 262144


def draw_geometry(key, part):
    key_height = jax.random.fold_in(key, 0)
    key_turn = jax.random.fold_in(key, 1)
    key_area = jax.random.fold_in(key, 3)
    height = jax.random.uniform(key_height, (ROWS,), jnp.float32, -1.0, 1.0)
    azimuth = jax.random.uniform(key_turn, (ROWS,), jnp.float32, -math.pi, math.pi)
    radius_xy = jnp.sqrt(jnp.maximum(1.0 - height * height, 0.0))
    normal = jnp.stack([radius_xy * jnp.cos(azimuth), radius_xy * jnp.sin(azimuth), height])
    radius = jnp.full((ROWS,), 6.0, jnp.float32)
    spread = jax.random.uniform(key_area, (ROWS,), jnp.float32, math.log(0.5), math.log(2.0))
    surface_area = jnp.exp(spread) * (0.05 / math.sqrt(LIVE_ALL))
    return jnp.concatenate([normal * radius[None, :], normal, surface_area[None, :]], axis=0).astype(jnp.float32)


def draw_counts(key, part):
    key_full, key_order, key_pairs, key_shift = jax.random.split(key, 4)
    full_device = jax.random.randint(key_full, (), 0, OWNERS)
    others = LIVE_OWN - CAP
    base_units = others // (OWNERS - 1)
    extra_units = others % (OWNERS - 1)
    ranking = jax.random.permutation(key_order, OWNERS - 1)
    units = base_units + (ranking < extra_units).astype(jnp.int32)
    pair_count = (OWNERS - 1) // 2
    picked = jax.random.permutation(key_pairs, OWNERS - 1)
    first_side = picked[:pair_count]
    second_side = picked[pair_count:2 * pair_count]
    limit = jnp.minimum(units[first_side] - 1, CAP - units[second_side])
    moving = jax.random.randint(key_shift, (pair_count,), 0, limit + 1)
    units = units.at[first_side].add(-moving).at[second_side].add(moving)
    lattice = jnp.arange(OWNERS)
    other_index = jnp.clip(lattice - (lattice > full_device).astype(jnp.int32), 0, OWNERS - 2)
    multiples = jnp.where(lattice == full_device, CAP, units[other_index])
    return (multiples * OWNERS).astype(jnp.int32)


def with_ends(values, key, smallest, high):
    extent = values.shape
    place = [jax.random.randint(jax.random.fold_in(key, axis), (), 0, extent[axis]) for axis in range(len(extent))]
    values = values.at[tuple(place)].set(smallest)
    longest = extent.index(max(extent))
    place[longest] = (place[longest] + 1) % extent[longest]
    return values.at[tuple(place)].set(high)


def levels(stream_key, extent, cuts, least, high):
    loudness = 1.0
    for dim, parts in cuts:
        steps = jax.random.uniform(jax.random.fold_in(jax.random.fold_in(stream_key, 6), dim), (parts,), jnp.float32, least / len(cuts), high / len(cuts))
        loudness = loudness * jnp.repeat(jnp.exp(steps), extent[dim] // parts).reshape((-1,) + (1,) * (len(extent) - 1 - dim))
    return loudness


def gaussian(stream_key, extent, width, reach, cuts=(), held_as=jnp.bfloat16):
    factor_of = levels(stream_key, extent, cuts, -0.22, 0.18) if cuts else 1.0
    array = jax.random.normal(stream_key, extent, jnp.float32) * width * factor_of
    return jnp.minimum(jnp.maximum(array, -reach), reach).astype(held_as)


def setup_inputs(seed: int = 0) -> dict:
    key_list = jax.random.split(jax.random.key(seed), 8)
    return {
        "cell_state": gaussian(key_list[0], (16, CELLS), 1.0, 6.0, ((1, 32),), jnp.float32),
        "geometry": draw_geometry(jax.random.fold_in(key_list[7], 71), 0),
        "surface_cell": with_ends(jax.random.randint(key_list[2], (ROWS,), 0, CELLS_DEV), jax.random.fold_in(key_list[2], 1), 0, CELLS_DEV - 1).astype(jnp.int32),
        "counts": draw_counts(jax.random.fold_in(key_list[7], 71), 0),
        "wavenumbers": jnp.clip(jnp.exp(jax.random.uniform(key_list[4], (F,), jnp.float32, math.log(8.0), math.log(24.0))), 8.0, 24.0),
        "target": gaussian(key_list[5], (F, 2, DIRS), 1.0, 6.0, (), jnp.float32),
        "direction_weight": jnp.clip(jnp.exp(jax.random.uniform(key_list[6], (DIRS,), jnp.float32, math.log(0.3), math.log(3.0))), 0.3, 3.0),
    }


GOLDEN = math.pi * (3.0 - math.sqrt(5.0))

def directions(count_dirs):
    lattice = jnp.arange(count_dirs).astype(jnp.float32)
    height = 1.0 - (2.0 * lattice + 1.0) / count_dirs
    radius_xy = jnp.sqrt(1.0 - height * height)
    azimuth = jnp.mod(lattice * GOLDEN, 2.0 * math.pi)
    return (radius_xy * jnp.cos(azimuth), radius_xy * jnp.sin(azimuth), height)

def kernel_block(points, wavenum, east_x, north_y, upward):
    phases = wavenum * (points[0][:, None] * east_x[None, :] + points[1][:, None] * north_y[None, :] + points[2][:, None] * upward[None, :])
    return jnp.concatenate([jnp.cos(phases), jnp.sin(phases)], axis=1).astype(jnp.bfloat16)

def source_rows(rows_block, level):
    surface_area = rows_block[22]
    normal = rows_block[19:22]
    pressure_real = rows_block[level] * surface_area
    pressure_imag = rows_block[4 + level] * surface_area
    return jnp.stack([rows_block[8 + level] * surface_area, normal[0] * pressure_real, normal[1] * pressure_real, normal[2] * pressure_real, rows_block[12 + level] * surface_area, normal[0] * pressure_imag, normal[1] * pressure_imag, normal[2] * pressure_imag]).astype(jnp.bfloat16)

def far_field_of(sums, wavenumbers, direction_basis):
    half_width = sums.shape[2] // 2
    cosine_part = sums[:, :, :half_width]
    sine_part = sums[:, :, half_width:]
    real_q = cosine_part[:, 0:4] + sine_part[:, 4:8]
    imag_q = cosine_part[:, 4:8] - sine_part[:, 0:4]
    real_z = lax.optimization_barrier(jnp.sum(direction_basis[None] * real_q, axis=1))
    imag_z = lax.optimization_barrier(jnp.sum(direction_basis[None] * imag_q, axis=1))
    wavenum = wavenumbers[:, None]
    return jnp.stack([-wavenum * imag_z, wavenum * real_z], axis=1)

def adjoint_weights(far_field, target, direction_weight, wavenumbers, direction_basis):
    count_dirs = far_field.shape[2]
    mismatch = far_field - target
    objective = jnp.sum(direction_weight * mismatch * mismatch) / count_dirs
    gradient = 2.0 * direction_weight * mismatch / count_dirs
    wavenum = wavenumbers[:, None]
    real_gz = wavenum * gradient[:, 1]
    imag_gz = -wavenum * gradient[:, 0]
    real_gq = direction_basis[None] * real_gz[:, None]
    imag_gq = direction_basis[None] * imag_gz[:, None]
    upper_half = jnp.concatenate([real_gq, -imag_gq], axis=2)
    lower_half = jnp.concatenate([imag_gq, real_gq], axis=2)
    return (objective, jnp.concatenate([upper_half, lower_half], axis=1).astype(jnp.bfloat16))

def adjoint_sources(products, normal):
    pressure_real = lax.optimization_barrier(jnp.sum(normal[None] * products[:, 1:4], axis=1))
    pressure_imag = lax.optimization_barrier(jnp.sum(normal[None] * products[:, 5:8], axis=1))
    return jnp.concatenate([pressure_real, pressure_imag, products[:, 0], products[:, 4]], axis=0)

def reference(cell_state, geometry, surface_cell, counts, wavenumbers, target, direction_weight):
    num_freqs = wavenumbers.shape[0]
    count_dirs = target.shape[2]
    total_rows = surface_cell.shape[0]
    row_index = jnp.arange(total_rows).astype(jnp.int32)
    device = row_index // ROWS_DEV
    living = row_index % ROWS_DEV < counts[device]
    cell_index = (device * CELLS_DEV + surface_cell).astype(jnp.int32)
    live_rank = jnp.cumsum(living.astype(jnp.int32)) - 1
    packed_slot = jnp.where(living, live_rank, LIVE_ALL).astype(jnp.int32)
    values = jnp.concatenate([cell_state[:, cell_index], geometry], axis=0)
    packed = jnp.zeros((23, LIVE_ALL), values.dtype).at[:, packed_slot].set(values, mode='drop')
    block_rows = math.gcd(LIVE_ALL, 4096)
    block_count = LIVE_ALL // block_rows
    blocks = packed.reshape(23, block_count, block_rows).transpose(1, 0, 2)
    east_x, north_y, upward = directions(count_dirs)
    direction_basis = jnp.stack([jnp.ones_like(east_x), east_x, north_y, upward])

    def forward_block(running, rows_block):
        products = [jnp.dot(source_rows(rows_block, level), kernel_block(rows_block[16:19], wavenumbers[level], east_x, north_y, upward), preferred_element_type=jnp.float32) for level in range(num_freqs)]
        return (running + jnp.stack(products), None)
    sums, _ = lax.scan(forward_block, jnp.zeros((num_freqs, 8, 2 * count_dirs), jnp.float32), blocks)
    far_field = far_field_of(sums, wavenumbers, direction_basis)
    objective, weights = adjoint_weights(far_field, target, direction_weight, wavenumbers, direction_basis)

    def adjoint_block(carry, rows_block):
        products = [lax.dot_general(weights[level], kernel_block(rows_block[16:19], wavenumbers[level], east_x, north_y, upward), (((1,), (1,)), ((), ())), preferred_element_type=jnp.float32) for level in range(num_freqs)]
        return (carry, adjoint_sources(jnp.stack(products), rows_block[19:22]))
    _, backward = lax.scan(adjoint_block, jnp.zeros((), jnp.float32), blocks)
    backward = backward.transpose(1, 0, 2).reshape(16, LIVE_ALL)
    per_row = backward[:, jnp.minimum(packed_slot, LIVE_ALL - 1)] * living.astype(backward.dtype)[None, :]
    cell_adjoint = jnp.zeros(cell_state.shape, backward.dtype).at[:, cell_index].add(per_row)
    return (far_field, objective, cell_adjoint)
```

```python
import functools
import math

import jax
import jax.numpy as jnp
import numpy as np
from jax import lax
from jax.experimental import pallas as pl
from jax.experimental.pallas import tpu as pltpu
from jax.sharding import PartitionSpec as P

GOLDEN = math.pi * (3.0 - math.sqrt(5.0))
AXES = ("gx", "gy")
F32 = jnp.float32
BF16 = jnp.bfloat16
LANES = 128
FREQS = 4
VMEM_BYTES = 48 * 2**20

SIN_K, SIN_A, SIN_B = 2.299546, 1.116939, 0.118212
COS_K, COS_A, COS_B = 3.583841, 0.682394, 0.186797


def direction_tables(count_dirs):
    lattice = np.arange(count_dirs).astype(np.float32)
    height = (np.float32(1.0) - (np.float32(2.0) * lattice + np.float32(1.0)) / np.float32(count_dirs)).astype(np.float32)
    radius_xy = np.sqrt(np.float32(1.0) - height * height).astype(np.float32)
    azimuth = np.mod(lattice * np.float32(GOLDEN), np.float32(2.0 * math.pi)).astype(np.float32)
    d = np.stack([radius_xy * np.cos(azimuth), radius_xy * np.sin(azimuth), height]).astype(np.float32)
    basis = np.concatenate([np.ones((1, count_dirs), np.float32), d, np.zeros((4, count_dirs), np.float32)])
    d1 = d.astype(jnp.bfloat16)
    d2 = (d - d1.astype(np.float32)).astype(jnp.bfloat16)
    d3 = (d - d1.astype(np.float32) - d2.astype(np.float32)).astype(jnp.bfloat16)
    parts = np.concatenate([d1, d1, d1, d2, d2, d3, d2, d3, np.zeros((8, count_dirs), d1.dtype)])
    return basis, np.concatenate([parts] * FREQS)


def bf16_parts(x):
    x1 = x.astype(BF16).astype(F32)
    x2 = (x - x1).astype(BF16).astype(F32)
    return x1, x2, x - x1 - x2


def gather_kernel(count_ref, cell_ref, rows_ref, out_ref, a1_ref, a2_ref, *, cap, owners, chunk):
    cells = cell_ref.shape[1]
    high = cells // 256
    for h in range(high):
        part = cell_ref[:, h * 256 : (h + 1) * 256]
        top = part.astype(BF16)
        a1_ref[h * 16 : (h + 1) * 16, :] = top
        a2_ref[h * 16 : (h + 1) * 16, :] = (part - top.astype(F32)).astype(BF16)
    live_slots = count_ref[0] // owners
    marker = live_slots.astype(F32)
    lane = lax.broadcasted_iota(jnp.int32, (1, LANES), 1)
    live = (lane % cap) < live_slots
    tiles = out_ref.shape[0]

    @pl.loop(0, tiles // chunk)
    def _(step):
        width = chunk * LANES
        base = step * chunk
        cell = jnp.concatenate([rows_ref[base + t, 7:8, :] for t in range(chunk)], axis=1)
        hi = jnp.floor(cell * (1.0 / 256.0))
        lo = cell - hi * 256.0
        level = lax.broadcasted_iota(jnp.int32, (256, width), 0).astype(F32)
        pick = jnp.where(level == lo, 1.0, 0.0).astype(BF16)
        found = jnp.dot(a1_ref[...], pick, preferred_element_type=F32) + jnp.dot(
            a2_ref[...], pick, preferred_element_type=F32
        )
        hi = jnp.broadcast_to(hi, (16, width))
        total = jnp.zeros((16, width), F32)
        for h in range(high):
            total = jnp.where(hi == float(h), found[h * 16 : (h + 1) * 16, :], total)
        for t in range(chunk):
            rows = rows_ref[base + t]
            out_ref[base + t, 0:16, :] = jnp.where(
                live, total[:, t * LANES : (t + 1) * LANES] * rows[6:7, :], 0.0
            )
            out_ref[base + t, 16:24, :] = jnp.where(live, rows, 0.0)
            out_ref[base + t, 23:24, :] = jnp.full((1, LANES), 1.0, F32) * marker


def forward_kernel(
    size_ref, start_ref, wave_ref, came_ref, parts_ref, basis_ref,
    t_ref, s_ref, far_ref, rows_ref, packed_ref, y_ref, src_ref,
):
    sources = came_ref.shape[0]
    live_own = rows_ref.shape[1]
    blocks = live_own // LANES
    width = far_ref.shape[1]

    @pl.when(pl.program_id(0) == 0)
    def _():
        packed_ref[...] = jnp.zeros(packed_ref.shape, F32)
        lane = lax.broadcasted_iota(jnp.int32, (24, LANES), 1)

        @pl.loop(0, sources)
        def _(s):
            offset = start_ref[s]
            base = offset // LANES
            shift = offset % LANES
            tile = jnp.where(lane < size_ref[s], came_ref[s], 0.0)
            tile = pltpu.roll(tile, shift, 1)
            packed_ref[base] += jnp.where(lane >= shift, tile, 0.0)
            packed_ref[base + 1] += jnp.where(lane >= shift, 0.0, tile)

        rows = jnp.concatenate([packed_ref[b] for b in range(blocks)], axis=1)
        rows_ref[...] = rows[16:24]
        point = rows[16:19]
        normal = rows[19:22]
        turned = []
        for f in range(FREQS):
            y1, y2, y3 = bf16_parts(point * (wave_ref[f] * (0.5 / math.pi)))
            turned += [y1, y2, y3, y1, y2, y1, y3, y2, jnp.zeros((8, live_own), F32)]
        turned = jnp.concatenate(turned, axis=0).T
        column = lax.broadcasted_iota(jnp.int32, (live_own, LANES), 1)
        for f in range(FREQS):
            mine = (column >= 32 * f) & (column < 32 * f + 32)
            y_ref[f] = jnp.where(mine, turned, 0.0).astype(BF16)
            real = jnp.concatenate([rows[8 + f : 9 + f], normal * rows[f : f + 1]], axis=0)
            imag = jnp.concatenate([rows[12 + f : 13 + f], normal * rows[4 + f : 5 + f]], axis=0)
            src_ref[f, 0] = jnp.concatenate([real, imag], axis=0).astype(BF16)
            src_ref[f, 1] = jnp.concatenate([imag, -real], axis=0).astype(BF16)

    piece = 256
    far = []
    for f in range(FREQS):
        total_t = jnp.zeros((8, width), F32)
        total_s = jnp.zeros((8, width), F32)
        for i in range(live_own // piece):
            at = slice(i * piece, (i + 1) * piece)
            turns = jnp.dot(y_ref[f, at, :], parts_ref[...], preferred_element_type=F32)
            t_val, s_val = half_angle(turns)
            t_ref[0, f, at, :] = t_val
            s_ref[0, f, at, :] = s_val
            total_t += jnp.dot(src_ref[f, 0, :, at], t_val, preferred_element_type=F32)
            total_s += jnp.dot(src_ref[f, 1, :, at], s_val, preferred_element_type=F32)
        whole = jnp.sum(src_ref[f, 0].astype(F32), axis=1, keepdims=True)
        q = whole - (2.0 * SIN_K * SIN_K) * total_t + (2.0 * SIN_K * COS_K) * total_s
        weighted = q * jnp.concatenate([basis_ref[0:4, :]] * 2, axis=0)
        real_z = jnp.sum(weighted[0:4], axis=0, keepdims=True)
        imag_z = jnp.sum(weighted[4:8], axis=0, keepdims=True)
        far += [imag_z * (-wave_ref[f]), real_z * wave_ref[f]]
    far_ref[...] = jnp.concatenate(far, axis=0)


def half_angle(turns):
    r = turns - jnp.round(turns)
    u = r * r
    v = u - SIN_A
    half_sin = (v * v + SIN_B) * r
    w = u - COS_A
    half_cos = w * w - COS_B
    return (half_sin * half_sin).astype(BF16), (half_sin * half_cos).astype(BF16)


def adjoint_kernel(
    size_ref, start_ref, wave_ref, far_ref, target_ref, weight_ref, basis_ref, rows_ref, t_ref, s_ref,
    out_ref, cost_ref, sum_ref, acc_ref, flat_ref, *, count_dirs,
):
    step = pl.program_id(0)
    live_own = rows_ref.shape[1]
    blocks = live_own // LANES
    mismatch = far_ref[...] - target_ref[...]
    weight = weight_ref[...]
    pull = weight * mismatch
    cost = pull * mismatch
    gradient = pull * (2.0 / count_dirs)
    basis = jnp.concatenate([basis_ref[0:4, :]] * 2, axis=0)

    @pl.when(step == 0)
    def _():
        acc_ref[...] = jnp.zeros(acc_ref.shape, F32)
        sum_ref[...] = jnp.zeros(sum_ref.shape, F32)

    sum_ref[...] += cost
    contract = (((1,), (1,)), ((), ()))
    for f in range(FREQS):
        real_gz = gradient[2 * f + 1 : 2 * f + 2] * wave_ref[f]
        imag_gz = gradient[2 * f : 2 * f + 1] * (-wave_ref[f])
        four = (4, real_gz.shape[1])
        real_gz = jnp.broadcast_to(real_gz, four)
        imag_gz = jnp.broadcast_to(imag_gz, four)
        for_cos = (basis * jnp.concatenate([real_gz, imag_gz], axis=0)).astype(BF16)
        for_sin = (basis * jnp.concatenate([-imag_gz, real_gz], axis=0)).astype(BF16)
        whole = jnp.sum(for_cos.astype(F32), axis=1, keepdims=True)
        part = lax.dot_general(for_cos, t_ref[0, f], contract, preferred_element_type=F32)
        other = lax.dot_general(for_sin, s_ref[0, f], contract, preferred_element_type=F32)
        acc_ref[f] += whole - (2.0 * SIN_K * SIN_K) * part + (2.0 * SIN_K * COS_K) * other

    @pl.when(step == pl.num_programs(0) - 1)
    def _():
        cost_ref[0] = jnp.sum(sum_ref[...]) / count_dirs
        normal = rows_ref[3:6]
        pressure_real, pressure_imag, velocity_real, velocity_imag = [], [], [], []
        for f in range(FREQS):
            got = acc_ref[f]
            pressure_real.append(jnp.sum(normal * got[1:4], axis=0, keepdims=True))
            pressure_imag.append(jnp.sum(normal * got[5:8], axis=0, keepdims=True))
            velocity_real.append(got[0:1])
            velocity_imag.append(got[4:5])
        flat = jnp.concatenate(pressure_real + pressure_imag + velocity_real + velocity_imag, axis=0)
        for b in range(blocks):
            flat_ref[b] = flat[:, b * LANES : (b + 1) * LANES]
        flat_ref[blocks] = jnp.zeros((16, LANES), F32)
        lane = lax.broadcasted_iota(jnp.int32, (16, LANES), 1)

        @pl.loop(0, out_ref.shape[0])
        def _(s):
            offset = start_ref[s]
            base = offset // LANES
            shift = offset % LANES
            back = (LANES - shift) % LANES
            first = pltpu.roll(flat_ref[base], back, 1)
            second = pltpu.roll(flat_ref[base + 1], back, 1)
            joined = jnp.where(lane < LANES - shift, first, second)
            out_ref[s] = jnp.where(lane < size_ref[s], joined, 0.0)


def scatter_kernel(value_ref, rows_ref, out_ref, *, chunk):
    tiles = value_ref.shape[0]
    high = out_ref.shape[1] // 256
    width = chunk * LANES
    contract = (((1,), (1,)), ((), ()))

    def body(step, total):
        base = step * chunk
        cell = jnp.concatenate([rows_ref[base + t, 7:8, :] for t in range(chunk)], axis=1)
        value = jnp.concatenate([value_ref[base + t] for t in range(chunk)], axis=1)
        hi = jnp.floor(cell * (1.0 / 256.0))
        lo = cell - hi * 256.0
        level = lax.broadcasted_iota(jnp.int32, (256, width), 0).astype(F32)
        pick = jnp.where(level == lo, 1.0, 0.0).astype(BF16)
        top = value.astype(BF16)
        rest = (value - top.astype(F32)).astype(BF16)
        hi = jnp.broadcast_to(hi, (16, width)).astype(BF16)
        zero = jnp.zeros((16, width), BF16)
        tops = jnp.concatenate([jnp.where(hi == float(h), top, zero) for h in range(high)], axis=0)
        rests = jnp.concatenate([jnp.where(hi == float(h), rest, zero) for h in range(high)], axis=0)
        total = total + lax.dot_general(tops, pick, contract, preferred_element_type=F32)
        return total + lax.dot_general(rests, pick, contract, preferred_element_type=F32)

    total = lax.fori_loop(0, tiles // chunk, body, jnp.zeros((high * 16, 256), F32))
    for h in range(high):
        out_ref[:, h * 256 : (h + 1) * 256] = total[h * 16 : (h + 1) * 16, :]


def smem():
    return pl.BlockSpec(memory_space=pltpu.SMEM)


def params():
    return pltpu.CompilerParams(vmem_limit_bytes=VMEM_BYTES)


def to_tiles(x, cap):
    owners, channels, _ = x.shape
    if cap == LANES:
        return x
    many = LANES // cap
    x = x.reshape(owners // many, many, channels, cap).transpose(0, 2, 1, 3)
    return x.reshape(owners // many, channels, LANES)


def from_tiles(x, cap):
    tiles, channels, _ = x.shape
    if cap == LANES:
        return x
    many = LANES // cap
    x = x.reshape(tiles, channels, many, cap).transpose(0, 2, 1, 3)
    return x.reshape(tiles * many, channels, cap)


def all_sum(x):
    for axis in AXES:
        size = lax.axis_size(axis)
        hop = 1
        while hop < size:
            x = x + lax.ppermute(x, axis, [(i, i ^ hop) for i in range(size)])
            hop *= 2
    return x


def on_device(cell_state, geometry, surface_cell, counts, wavenumbers, target, direction_weight):
    owners = lax.axis_size(AXES)
    rows_dev = surface_cell.shape[0]
    cells = cell_state.shape[1]
    cap = rows_dev // owners
    live_own = rows_dev // 4
    count_dirs = target.shape[2]
    tiles = rows_dev // LANES
    high = cells // 256
    basis, parts = direction_tables(count_dirs)
    basis, parts = jnp.asarray(basis), jnp.asarray(parts)

    rows = jnp.concatenate([geometry, surface_cell.astype(F32)[None, :]], axis=0)
    rows = to_tiles(rows.reshape(8, cap, owners).transpose(2, 0, 1), cap)
    outgoing = pl.pallas_call(
        functools.partial(gather_kernel, cap=cap, owners=owners, chunk=4),
        in_specs=[smem(), pl.BlockSpec(memory_space=pltpu.VMEM), pl.BlockSpec(memory_space=pltpu.VMEM)],
        out_shape=jax.ShapeDtypeStruct((tiles, 24, LANES), F32),
        scratch_shapes=[pltpu.VMEM((high * 16, 256), BF16), pltpu.VMEM((high * 16, 256), BF16)],
        compiler_params=params(),
        name="gather_rows",
    )(counts, cell_state, rows)
    outgoing = from_tiles(outgoing, cap)
    came = lax.all_to_all(outgoing, AXES, split_axis=0, concat_axis=0, tiled=True)
    size = came[:, 23, 0].astype(jnp.int32)
    start = jnp.cumsum(size) - size
    if cap < LANES:
        came = jnp.pad(came, ((0, 0), (0, 0), (0, LANES - cap)))

    width = 256
    grid = count_dirs // width
    block = pl.BlockSpec((1, FREQS, live_own, width), lambda i: (i, 0, 0, 0))
    stored = jax.ShapeDtypeStruct((grid, FREQS, live_own, width), BF16)
    by_dir = lambda i: (0, i)
    whole2 = lambda i: (0, 0)
    t_all, s_all, far, kept = pl.pallas_call(
        forward_kernel,
        grid=(grid,),
        in_specs=[
            smem(), smem(), smem(),
            pl.BlockSpec((owners, 24, LANES), lambda i: (0, 0, 0)),
            pl.BlockSpec((32 * FREQS, width), by_dir),
            pl.BlockSpec((8, width), by_dir),
        ],
        out_specs=[block, block, pl.BlockSpec((2 * FREQS, width), by_dir), pl.BlockSpec((8, live_own), whole2)],
        out_shape=[
            stored, stored,
            jax.ShapeDtypeStruct((2 * FREQS, count_dirs), F32),
            jax.ShapeDtypeStruct((8, live_own), F32),
        ],
        scratch_shapes=[
            pltpu.VMEM((live_own // LANES + 1, 24, LANES), F32),
            pltpu.VMEM((FREQS, live_own, LANES), BF16),
            pltpu.VMEM((FREQS, 2, 8, live_own), BF16),
        ],
        compiler_params=params(),
        name="forward",
    )(size, start, wavenumbers, came, parts, basis)

    far = all_sum(far)

    back, objective = pl.pallas_call(
        functools.partial(adjoint_kernel, count_dirs=count_dirs),
        grid=(grid,),
        in_specs=[
            smem(), smem(), smem(),
            pl.BlockSpec((2 * FREQS, width), by_dir),
            pl.BlockSpec((2 * FREQS, width), by_dir),
            pl.BlockSpec((1, width), by_dir),
            pl.BlockSpec((8, width), by_dir),
            pl.BlockSpec((8, live_own), whole2),
            block, block,
        ],
        out_specs=[pl.BlockSpec((owners, 16, LANES), lambda i: (0, 0, 0)), smem()],
        out_shape=[jax.ShapeDtypeStruct((owners, 16, LANES), F32), jax.ShapeDtypeStruct((1,), F32)],
        scratch_shapes=[
            pltpu.VMEM((2 * FREQS, width), F32),
            pltpu.VMEM((FREQS, 8, live_own), F32),
            pltpu.VMEM((live_own // LANES + 1, 16, LANES), F32),
        ],
        compiler_params=params(),
        name="adjoint",
    )(
        size, start, wavenumbers, far, target.reshape(2 * FREQS, count_dirs),
        direction_weight.reshape(1, count_dirs), basis, kept, t_all, s_all,
    )
    returned = lax.all_to_all(back[:, :, :cap], AXES, split_axis=0, concat_axis=0, tiled=True)
    cell_adjoint = pl.pallas_call(
        functools.partial(scatter_kernel, chunk=4),
        in_specs=[pl.BlockSpec(memory_space=pltpu.VMEM), pl.BlockSpec(memory_space=pltpu.VMEM)],
        out_shape=jax.ShapeDtypeStruct(cell_state.shape, F32),
        compiler_params=params(),
        name="scatter_rows",
    )(to_tiles(returned, cap), rows)
    return (far.reshape(FREQS, 2, count_dirs), objective[0], cell_adjoint)


def solution(mesh):
    placed = (
        P(None, AXES),
        P(None, AXES),
        P(AXES),
        P(AXES),
        P(),
        P(),
        P(),
    )
    return jax.shard_map(
        on_device,
        mesh=mesh,
        in_specs=placed,
        out_specs=(P(), P(), P(None, AXES)),
        check_vma=False,
    )
```

```python
import functools
import math

import jax
import jax.numpy as jnp
import numpy as np
from jax import lax
from jax.experimental import pallas as pl
from jax.experimental.pallas import tpu as pltpu
from jax.sharding import PartitionSpec as P

GOLDEN = math.pi * (3.0 - math.sqrt(5.0))
AXES = ("gx", "gy")
F32 = jnp.float32
BF16 = jnp.bfloat16
LANES = 128
FREQS = 4
VMEM_BYTES = 24 * 2**20
PIECE = 1024

SIN_K, SIN_A, SIN_B = 2.299546, 1.116939, 0.118212
COS_K, COS_A, COS_B = 3.583841, 0.682394, 0.186797
COS_SCALE = 2.0 * SIN_K * SIN_K
SIN_SCALE = 2.0 * SIN_K * COS_K


def direction_tables(count_dirs):
    lattice = np.arange(count_dirs).astype(np.float32)
    height = (np.float32(1.0) - (np.float32(2.0) * lattice + np.float32(1.0)) / np.float32(count_dirs)).astype(np.float32)
    radius_xy = np.sqrt(np.float32(1.0) - height * height).astype(np.float32)
    azimuth = np.mod(lattice * np.float32(GOLDEN), np.float32(2.0 * math.pi)).astype(np.float32)
    d = np.stack([radius_xy * np.cos(azimuth), radius_xy * np.sin(azimuth), height]).astype(np.float32)
    basis = np.concatenate([np.ones((1, count_dirs), np.float32), d, np.zeros((4, count_dirs), np.float32)])
    d1 = d.astype(jnp.bfloat16)
    d2 = (d - d1.astype(np.float32)).astype(jnp.bfloat16)
    d3 = (d - d1.astype(np.float32) - d2.astype(np.float32)).astype(jnp.bfloat16)
    parts = np.concatenate([d1, d1, d1, d2, d2, d3, d2, d3, np.zeros((8, count_dirs), d1.dtype)])
    return basis, np.concatenate([parts] * FREQS)


def bf16_parts(x):
    x1 = x.astype(BF16).astype(F32)
    x2 = (x - x1).astype(BF16).astype(F32)
    return x1, x2, x - x1 - x2


def gather_kernel(cell_ref, index_ref, rows_ref, out_ref, a1_ref, a2_ref, *, chunk):
    cells = cell_ref.shape[1]
    high = cells // 256
    for h in range(high):
        part = cell_ref[:, h * 256 : (h + 1) * 256]
        top = part.astype(BF16)
        a1_ref[h * 16 : (h + 1) * 16, :] = top
        a2_ref[h * 16 : (h + 1) * 16, :] = (part - top.astype(F32)).astype(BF16)
    tiles = out_ref.shape[0]

    @pl.loop(0, tiles // chunk)
    def _(step):
        width = chunk * LANES
        base = step * chunk
        cell = jnp.concatenate([index_ref[base + t] for t in range(chunk)], axis=1)
        hi = lax.shift_right_logical(cell, 8)
        lo = cell & 255
        level = lax.broadcasted_iota(jnp.int32, (256, width), 0)
        pick = jnp.where(level == lo, 1.0, 0.0).astype(BF16)
        found = jnp.dot(a1_ref[...], pick, preferred_element_type=F32) + jnp.dot(
            a2_ref[...], pick, preferred_element_type=F32
        )
        hi = jnp.broadcast_to(hi, (16, width))
        total = jnp.zeros((16, width), F32)
        for h in range(high):
            total = jnp.where(hi == h, found[h * 16 : (h + 1) * 16, :], total)
        for t in range(chunk):
            out_ref[base + t] = total[:, t * LANES : (t + 1) * LANES] * rows_ref[base + t, 6:7, :]


def pack_rows(ends_ref, came_ref, packed_ref):
    sources, channels, _ = came_ref.shape
    lane = lax.broadcasted_iota(jnp.int32, (channels, LANES), 1)

    def body(s, carry):
        offset = ends_ref[0, s]
        base = offset // LANES
        shift = offset % LANES
        tile = pltpu.roll(came_ref[s], shift, 1)
        pltpu.store(packed_ref.at[base], tile, mask=lane >= shift)
        pltpu.store(packed_ref.at[base + 1], tile, mask=lane < shift)
        return carry

    lax.fori_loop(0, sources, body, 0, unroll=8)
    return jnp.concatenate([packed_ref[b] for b in range(packed_ref.shape[0] - 1)], axis=1)


def half_angle(turns):
    r = turns - jnp.round(turns)
    u = r * r
    v = u - SIN_A
    half_sin = (v * v + SIN_B) * r
    w = u - COS_A
    half_cos = w * w - COS_B
    return (half_sin * half_sin).astype(BF16), (half_sin * half_cos).astype(BF16)


def masked_parts(parts_ref, f):
    parts = parts_ref[...]
    level = lax.broadcasted_iota(jnp.int32, parts.shape, 0)
    return jnp.where((level >= 32 * f) & (level < 32 * f + 32), parts.astype(F32), 0.0).astype(BF16)


def phase_kernel(ends_ref, wave_ref, came_ref, parts_ref, t_ref, s_ref, rows_ref, y_ref, packed_ref):
    live_own = rows_ref.shape[1]

    @pl.when(pl.program_id(0) == 0)
    def _():
        rows = pack_rows(ends_ref, came_ref, packed_ref)
        rows_ref[...] = rows
        turned = []
        for f in range(FREQS):
            y1, y2, y3 = bf16_parts(rows[0:3] * (wave_ref[f] * (0.5 / math.pi)))
            turned += [y1, y2, y3, y1, y2, y1, y3, y2, jnp.zeros((8, live_own), F32)]
        y_ref[...] = jnp.concatenate(turned, axis=0).T.astype(BF16)

    for f in range(FREQS):
        parts = masked_parts(parts_ref, f)
        for i in range(live_own // PIECE):
            at = slice(i * PIECE, (i + 1) * PIECE)
            turns = jnp.dot(y_ref[at, :], parts, preferred_element_type=F32)
            t_ref[0, f, at, :], s_ref[0, f, at, :] = half_angle(turns)


def radiate_kernel(
    ends_ref, wave_ref, came_ref, rows_ref, y_ref, parts_ref, basis_ref, first_t_ref, first_s_ref,
    far_ref, t_ref, s_ref, packed_ref, src_ref, t_sem, s_sem,
):
    live_own = rows_ref.shape[1]
    step = pl.program_id(0)
    steps = pl.num_programs(0)
    half, _, _, width = first_t_ref.shape

    def fetch(i):
        return (
            pltpu.make_async_copy(first_t_ref.at[i], t_ref.at[i], t_sem.at[i]),
            pltpu.make_async_copy(first_s_ref.at[i], s_ref.at[i], s_sem.at[i]),
        )

    @pl.when(step == 0)
    def _():
        for i in range(half):
            for copy in fetch(i):
                copy.start()
        rows = pack_rows(ends_ref, came_ref, packed_ref)
        normal = rows_ref[3:6]
        for f in range(FREQS):
            real = jnp.concatenate([rows[8 + f : 9 + f], normal * rows[f : f + 1]], axis=0)
            imag = jnp.concatenate([rows[12 + f : 13 + f], normal * rows[4 + f : 5 + f]], axis=0)
            src_ref[f, 0] = jnp.concatenate([real, imag], axis=0).astype(BF16)
            src_ref[f, 1] = jnp.concatenate([imag, -real], axis=0).astype(BF16)

    def project(f, total_t, total_s, basis):
        whole = jnp.sum(src_ref[f, 0].astype(F32), axis=1, keepdims=True)
        q = whole - COS_SCALE * total_t + SIN_SCALE * total_s
        weighted = q * jnp.concatenate([basis] * 2, axis=0)
        real_z = jnp.sum(weighted[0:4], axis=0, keepdims=True)
        imag_z = jnp.sum(weighted[4:8], axis=0, keepdims=True)
        return [imag_z * (-wave_ref[f]), real_z * wave_ref[f]]

    first, second = (pl.ds(pl.multiple_of(i * width, width), width) for i in (step, steps + step))
    basis1 = basis_ref[0:4, first]
    basis2 = basis_ref[0:4, second]
    far1, far2 = [], []
    for copy in fetch(step):
        copy.wait()
    for f in range(FREQS):
        total_t = jnp.dot(src_ref[f, 0], t_ref[step, f], preferred_element_type=F32)
        total_s = jnp.dot(src_ref[f, 1], s_ref[step, f], preferred_element_type=F32)
        far1 += project(f, total_t, total_s, basis1)
        parts = masked_parts(parts_ref, f)
        for i in range(live_own // PIECE):
            at = slice(i * PIECE, (i + 1) * PIECE)
            turns = jnp.dot(y_ref[at, :], parts, preferred_element_type=F32)
            t_ref[steps + step, f, at, :], s_ref[steps + step, f, at, :] = half_angle(turns)
        total_t = jnp.dot(src_ref[f, 0], t_ref[steps + step, f], preferred_element_type=F32)
        total_s = jnp.dot(src_ref[f, 1], s_ref[steps + step, f], preferred_element_type=F32)
        far2 += project(f, total_t, total_s, basis2)
    far_ref[:, first] = jnp.concatenate(far1, axis=0)
    far_ref[:, second] = jnp.concatenate(far2, axis=0)


def adjoint_kernel(
    ends_ref, wave_ref, far_ref, target_ref, weight_ref, basis_ref, rows_ref,
    t_ref, s_ref, out_ref, cost_ref, _t, _s, flat_ref,
):
    live_own = rows_ref.shape[1]
    blocks = live_own // LANES
    count_dirs = far_ref.shape[1]
    width = t_ref.shape[3]
    mismatch = far_ref[...] - jnp.concatenate([target_ref[f] for f in range(FREQS)], axis=0)
    pull = weight_ref[...] * mismatch
    cost_ref[0] = jnp.sum(pull * mismatch) / count_dirs
    gradient = pull * (2.0 / count_dirs)
    basis = jnp.concatenate([basis_ref[0:4, :]] * 2, axis=0)
    contract = (((1,), (1,)), ((), ()))
    normal = rows_ref[3:6]
    pressure_real, pressure_imag, velocity_real, velocity_imag = [], [], [], []
    for f in range(FREQS):
        real_gz = jnp.broadcast_to(gradient[2 * f + 1 : 2 * f + 2] * wave_ref[f], (4, count_dirs))
        imag_gz = jnp.broadcast_to(gradient[2 * f : 2 * f + 1] * (-wave_ref[f]), (4, count_dirs))
        for_cos = (basis * jnp.concatenate([real_gz, imag_gz], axis=0)).astype(BF16)
        for_sin = (basis * jnp.concatenate([-imag_gz, real_gz], axis=0)).astype(BF16)
        whole = jnp.sum(for_cos.astype(F32), axis=1, keepdims=True)
        total_t = jnp.zeros((8, live_own), F32)
        total_s = jnp.zeros((8, live_own), F32)
        for i in range(t_ref.shape[0]):
            at = slice(i * width, (i + 1) * width)
            total_t += lax.dot_general(for_cos[:, at], t_ref[i, f], contract, preferred_element_type=F32)
            total_s += lax.dot_general(for_sin[:, at], s_ref[i, f], contract, preferred_element_type=F32)
        got = whole - COS_SCALE * total_t + SIN_SCALE * total_s
        pressure_real.append(jnp.sum(normal * got[1:4], axis=0, keepdims=True))
        pressure_imag.append(jnp.sum(normal * got[5:8], axis=0, keepdims=True))
        velocity_real.append(got[0:1])
        velocity_imag.append(got[4:5])
    flat = jnp.concatenate(pressure_real + pressure_imag + velocity_real + velocity_imag, axis=0)
    for b in range(blocks):
        flat_ref[b] = flat[:, b * LANES : (b + 1) * LANES]
    flat_ref[blocks] = jnp.zeros((16, LANES), F32)
    lane = lax.broadcasted_iota(jnp.int32, (16, LANES), 1)

    def body(s, carry):
        offset = ends_ref[0, s]
        base = offset // LANES
        shift = offset % LANES
        back = (LANES - shift) % LANES
        joined = jnp.where(lane >= shift, flat_ref[base], flat_ref[base + 1])
        joined = pltpu.roll(joined, back, 1)
        out_ref[s] = jnp.where(lane < ends_ref[1, s], joined, 0.0)
        return carry

    lax.fori_loop(0, out_ref.shape[0], body, 0, unroll=8)


def scatter_kernel(value_ref, index_ref, out_ref, *, chunk):
    tiles = value_ref.shape[0]
    high = out_ref.shape[1] // 256
    width = chunk * LANES
    contract = (((1,), (1,)), ((), ()))

    def body(step, total):
        base = step * chunk
        cell = jnp.concatenate([index_ref[base + t] for t in range(chunk)], axis=1)
        value = jnp.concatenate([value_ref[base + t] for t in range(chunk)], axis=1)
        hi = lax.shift_right_logical(cell, 8)
        lo = cell & 255
        level = lax.broadcasted_iota(jnp.int32, (256, width), 0)
        pick = jnp.where(level == lo, 1.0, 0.0).astype(BF16)
        top = value.astype(BF16)
        rest = (value - top.astype(F32)).astype(BF16)
        hi = jnp.broadcast_to(hi, (16, width)).astype(F32).astype(BF16)
        zero = jnp.zeros((16, width), BF16)
        tops = jnp.concatenate([jnp.where(hi == float(h), top, zero) for h in range(high)], axis=0)
        rests = jnp.concatenate([jnp.where(hi == float(h), rest, zero) for h in range(high)], axis=0)
        total = total + lax.dot_general(tops, pick, contract, preferred_element_type=F32)
        return total + lax.dot_general(rests, pick, contract, preferred_element_type=F32)

    total = lax.fori_loop(0, tiles // chunk, body, jnp.zeros((high * 16, 256), F32))
    for h in range(high):
        out_ref[:, h * 256 : (h + 1) * 256] = total[h * 16 : (h + 1) * 16, :]


def smem():
    return pl.BlockSpec(memory_space=pltpu.SMEM)


def params():
    return pltpu.CompilerParams(vmem_limit_bytes=VMEM_BYTES)


def to_tiles(x, cap):
    owners, channels, _ = x.shape
    if cap == LANES:
        return x
    many = LANES // cap
    x = x.reshape(owners // many, many, channels, cap).transpose(0, 2, 1, 3)
    return x.reshape(owners // many, channels, LANES)


def from_tiles(x, cap):
    tiles, channels, _ = x.shape
    if cap == LANES:
        return x
    many = LANES // cap
    x = x.reshape(tiles, channels, many, cap).transpose(0, 2, 1, 3)
    return x.reshape(tiles * many, channels, cap)


def all_sum(x):
    gx, gy = (lax.axis_size(axis) for axis in AXES)
    low = gy.bit_length() - 1
    rest = [b for b in range((gx * gy).bit_length() - 1) if b != low]
    rounds = [[low]]
    if low % 2:
        rounds.append([rest.pop(0), rest.pop(-1)])
    rounds += [rest[i : i + 2] for i in range(0, len(rest), 2)]
    for bits in rounds:
        masks = [sum(1 << b for k, b in enumerate(bits) if code >> k & 1) for code in range(1, 1 << len(bits))]
        came = [lax.ppermute(x, AXES, [(i, i ^ m) for i in range(gx * gy)]) for m in masks]
        if len(came) == 1:
            x = x + came[0]
        else:
            x = (x + came[0]) + (came[1] + came[2])
    return x


def on_device(cell_state, geometry, surface_cell, counts, wavenumbers, target, direction_weight):
    owners = lax.axis_size(AXES)
    rows_dev = surface_cell.shape[0]
    cells = cell_state.shape[1]
    cap = rows_dev // owners
    live_own = rows_dev // 4
    count_dirs = target.shape[2]
    tiles = rows_dev // LANES
    high = cells // 256
    basis, parts = direction_tables(count_dirs)
    basis, parts = jnp.asarray(basis), jnp.asarray(parts)
    vmem = pl.BlockSpec(memory_space=pltpu.VMEM)

    share = (counts // owners).astype(F32)
    rows = jnp.concatenate([geometry, jnp.broadcast_to(share[None, :], (1, rows_dev))], axis=0)
    rows = rows.reshape(8, cap, owners).transpose(2, 0, 1)
    came = lax.all_to_all(rows, AXES, split_axis=0, concat_axis=0, tiled=True)
    index = to_tiles(surface_cell.reshape(cap, owners).T.reshape(owners, 1, cap), cap)
    outgoing = pl.pallas_call(
        functools.partial(gather_kernel, chunk=4),
        in_specs=[vmem, vmem, vmem],
        out_shape=jax.ShapeDtypeStruct((tiles, 16, LANES), F32),
        scratch_shapes=[pltpu.VMEM((high * 16, 256), BF16), pltpu.VMEM((high * 16, 256), BF16)],
        compiler_params=params(),
        name="gather_rows",
    )(cell_state, index, to_tiles(rows, cap))
    values = lax.all_to_all(from_tiles(outgoing, cap), AXES, split_axis=0, concat_axis=0, tiled=True)
    marks = np.stack([np.tril(np.ones((owners, owners), np.float32), -1), np.eye(owners, dtype=np.float32)])
    ends = jnp.sum(came[:, 7, 0] * marks, axis=2).astype(jnp.int32)
    if cap < LANES:
        came = jnp.pad(came, ((0, 0), (0, 0), (0, LANES - cap)))
        values = jnp.pad(values, ((0, 0), (0, 0), (0, LANES - cap)))

    parts, basis, came, values = (pltpu.with_memory_space_constraint(x, pltpu.HBM) for x in (parts, basis, came, values))
    width = 256
    half = count_dirs // width // 2
    packs = live_own // LANES + 1
    first = pltpu.HBM((half, FREQS, live_own, width), BF16)
    held = pltpu.VMEM((2 * half, FREQS, live_own, width), BF16)
    by_dir = lambda i: (0, i)
    block = pl.BlockSpec((1, FREQS, live_own, width), lambda i: (i, 0, 0, 0))
    first_t, first_s, kept, turned = pl.pallas_call(
        phase_kernel,
        grid=(half,),
        in_specs=[smem(), smem(), vmem, pl.BlockSpec((32 * FREQS, width), by_dir)],
        out_specs=[block, block, vmem, vmem],
        out_shape=[
            first, first,
            pltpu.HBM((8, live_own), F32),
            pltpu.HBM((live_own, 32 * FREQS), BF16),
        ],
        scratch_shapes=[pltpu.VMEM((packs, 8, LANES), F32)],
        compiler_params=params(),
        name="phases",
    )(ends, wavenumbers, came, parts)

    hbm = pl.BlockSpec(memory_space=pltpu.HBM)
    far, t_all, s_all = pl.pallas_call(
        radiate_kernel,
        grid=(half,),
        in_specs=[
            smem(), smem(), vmem, vmem, vmem,
            pl.BlockSpec((32 * FREQS, width), lambda i: (0, half + i)),
            vmem, hbm, hbm,
        ],
        out_specs=[vmem] * 3,
        out_shape=[jax.ShapeDtypeStruct((2 * FREQS, count_dirs), F32), held, held],
        scratch_shapes=[
            pltpu.VMEM((packs, 16, LANES), F32),
            pltpu.VMEM((FREQS, 2, 8, live_own), BF16),
            pltpu.SemaphoreType.DMA((half,)),
            pltpu.SemaphoreType.DMA((half,)),
        ],
        compiler_params=params(),
        name="radiate",
    )(ends, wavenumbers, values, kept, turned, parts, basis, first_t, first_s)

    far = all_sum(far)

    back, objective = pl.pallas_call(
        adjoint_kernel,
        in_specs=[smem(), smem()] + [vmem] * 7,
        out_specs=[vmem, smem(), vmem, vmem],
        out_shape=[
            jax.ShapeDtypeStruct((owners, 16, LANES), F32),
            jax.ShapeDtypeStruct((1,), F32),
            held, held,
        ],
        input_output_aliases={7: 2, 8: 3},
        scratch_shapes=[pltpu.VMEM((packs, 16, LANES), F32)],
        compiler_params=params(),
        name="adjoint",
    )(
        ends, wavenumbers, far, target, direction_weight.reshape(1, count_dirs), basis, kept, t_all, s_all,
    )[:2]
    returned = lax.all_to_all(back[:, :, :cap], AXES, split_axis=0, concat_axis=0, tiled=True)
    cell_adjoint = pl.pallas_call(
        functools.partial(scatter_kernel, chunk=4),
        in_specs=[vmem, vmem],
        out_shape=jax.ShapeDtypeStruct(cell_state.shape, F32),
        compiler_params=params(),
        name="scatter_rows",
    )(to_tiles(returned, cap), index)
    return (far.reshape(FREQS, 2, count_dirs), objective[0], cell_adjoint)


def solution(mesh):
    placed = (
        P(None, AXES),
        P(None, AXES),
        P(AXES),
        P(AXES),
        P(),
        P(),
        P(),
    )
    return jax.shard_map(
        on_device,
        mesh=mesh,
        in_specs=placed,
        out_specs=(P(), P(), P(None, AXES)),
        check_vma=False,
    )
```

```python
import functools
import math

import jax
import jax.numpy as jnp
import numpy as np
from jax import lax
from jax.experimental import pallas as pl
from jax.experimental.pallas import tpu as pltpu
from jax.sharding import PartitionSpec as P

GOLDEN = math.pi * (3.0 - math.sqrt(5.0))
AXES = ("gx", "gy")
F32 = jnp.float32
BF16 = jnp.bfloat16
LANES = 128
FREQS = 4
VMEM_BYTES = 24 * 2**20
PIECE = 1024

SIN_K, SIN_A, SIN_B = 2.299546, 1.116939, 0.118212
COS_K, COS_A, COS_B = 3.583841, 0.682394, 0.186797
COS_SCALE = 2.0 * SIN_K * SIN_K
SIN_SCALE = 2.0 * SIN_K * COS_K


def direction_tables(count_dirs):
    lattice = np.arange(count_dirs).astype(np.float32)
    height = (np.float32(1.0) - (np.float32(2.0) * lattice + np.float32(1.0)) / np.float32(count_dirs)).astype(np.float32)
    radius_xy = np.sqrt(np.float32(1.0) - height * height).astype(np.float32)
    azimuth = np.mod(lattice * np.float32(GOLDEN), np.float32(2.0 * math.pi)).astype(np.float32)
    d = np.stack([radius_xy * np.cos(azimuth), radius_xy * np.sin(azimuth), height]).astype(np.float32)
    basis = np.concatenate([np.ones((1, count_dirs), np.float32), d, np.zeros((4, count_dirs), np.float32)])
    d1 = d.astype(jnp.bfloat16)
    d2 = (d - d1.astype(np.float32)).astype(jnp.bfloat16)
    d3 = (d - d1.astype(np.float32) - d2.astype(np.float32)).astype(jnp.bfloat16)
    parts = np.concatenate([d1, d1, d1, d2, d2, d3, d2, d3, np.zeros((8, count_dirs), d1.dtype)])
    return basis, np.concatenate([parts] * FREQS)


def bf16_parts(x):
    x1 = x.astype(BF16).astype(F32)
    x2 = (x - x1).astype(BF16).astype(F32)
    return x1, x2, x - x1 - x2


def gather_kernel(cell_ref, index_ref, rows_ref, out_ref, a1_ref, a2_ref, *, chunk):
    cells = cell_ref.shape[1]
    high = cells // 256
    for h in range(high):
        part = cell_ref[:, h * 256 : (h + 1) * 256]
        top = part.astype(BF16)
        a1_ref[h * 16 : (h + 1) * 16, :] = top
        a2_ref[h * 16 : (h + 1) * 16, :] = (part - top.astype(F32)).astype(BF16)
    tiles = out_ref.shape[0]

    for step in range(tiles // chunk):
        width = chunk * LANES
        base = step * chunk
        cell = jnp.concatenate([index_ref[base + t] for t in range(chunk)], axis=1)
        hi = lax.shift_right_logical(cell, 8)
        lo = cell & 255
        level = lax.broadcasted_iota(jnp.int32, (256, width), 0)
        pick = jnp.where(level == lo, 1.0, 0.0).astype(BF16)
        found = jnp.dot(a1_ref[...], pick, preferred_element_type=F32) + jnp.dot(
            a2_ref[...], pick, preferred_element_type=F32
        )
        hi = jnp.broadcast_to(hi, (16, width))
        total = jnp.zeros((16, width), F32)
        for h in range(high):
            total = jnp.where(hi == h, found[h * 16 : (h + 1) * 16, :], total)
        for t in range(chunk):
            out_ref[base + t] = total[:, t * LANES : (t + 1) * LANES] * rows_ref[base + t, 6:7, :]


def pack_rows(ends_ref, came_ref, packed_ref):
    sources, channels, _ = came_ref.shape
    lane = lax.broadcasted_iota(jnp.int32, (channels, LANES), 1)

    def body(s, carry):
        offset = ends_ref[0, s]
        base = offset // LANES
        shift = offset % LANES
        tile = pltpu.roll(came_ref[s], shift, 1)
        pltpu.store(packed_ref.at[base], tile, mask=lane >= shift)
        pltpu.store(packed_ref.at[base + 1], tile, mask=lane < shift)
        return carry

    lax.fori_loop(0, sources, body, 0, unroll=8)
    return jnp.concatenate([packed_ref[b] for b in range(packed_ref.shape[0] - 1)], axis=1)


def half_angle(turns):
    r = turns - jnp.round(turns)
    u = r * r
    v = u - SIN_A
    half_sin = (v * v + SIN_B) * r
    w = u - COS_A
    half_cos = w * w - COS_B
    return (half_sin * half_sin).astype(BF16), (half_sin * half_cos).astype(BF16)


def masked_parts(parts_ref, f):
    parts = parts_ref[...]
    level = lax.broadcasted_iota(jnp.int32, parts.shape, 0)
    return jnp.where((level >= 32 * f) & (level < 32 * f + 32), parts.astype(F32), 0.0).astype(BF16)


def phase_kernel(ends_ref, wave_ref, came_ref, parts_ref, t_ref, s_ref, rows_ref, y_ref, packed_ref):
    live_own = rows_ref.shape[1]

    @pl.when(pl.program_id(0) == 0)
    def _():
        rows = pack_rows(ends_ref, came_ref, packed_ref)
        rows_ref[...] = rows
        turned = []
        for f in range(FREQS):
            y1, y2, y3 = bf16_parts(rows[0:3] * (wave_ref[f] * (0.5 / math.pi)))
            turned += [y1, y2, y3, y1, y2, y1, y3, y2, jnp.zeros((8, live_own), F32)]
        y_ref[...] = jnp.concatenate(turned, axis=0).T.astype(BF16)

    for f in range(FREQS):
        parts = masked_parts(parts_ref, f)
        for i in range(live_own // PIECE):
            at = slice(i * PIECE, (i + 1) * PIECE)
            turns = jnp.dot(y_ref[at, :], parts, preferred_element_type=F32)
            t_ref[0, f, at, :], s_ref[0, f, at, :] = half_angle(turns)


def radiate_kernel(
    ends_ref, wave_ref, came_ref, rows_ref, y_ref, parts_ref, basis_ref, first_t_ref, first_s_ref,
    far_ref, t_ref, s_ref, packed_ref, src_ref, t_sem, s_sem,
):
    live_own = rows_ref.shape[1]
    step = pl.program_id(0)
    steps = pl.num_programs(0)
    half, _, _, width = first_t_ref.shape

    def fetch(i):
        return (
            pltpu.make_async_copy(first_t_ref.at[i], t_ref.at[i], t_sem.at[i]),
            pltpu.make_async_copy(first_s_ref.at[i], s_ref.at[i], s_sem.at[i]),
        )

    @pl.when(step == 0)
    def _():
        for i in range(half):
            for copy in fetch(i):
                copy.start()
        rows = pack_rows(ends_ref, came_ref, packed_ref)
        normal = rows_ref[3:6]
        for f in range(FREQS):
            real = jnp.concatenate([rows[8 + f : 9 + f], normal * rows[f : f + 1]], axis=0)
            imag = jnp.concatenate([rows[12 + f : 13 + f], normal * rows[4 + f : 5 + f]], axis=0)
            src_ref[f, 0] = jnp.concatenate([real, imag], axis=0).astype(BF16)
            src_ref[f, 1] = jnp.concatenate([imag, -real], axis=0).astype(BF16)

    def project(f, total_t, total_s, basis):
        whole = jnp.sum(src_ref[f, 0].astype(F32), axis=1, keepdims=True)
        q = whole - COS_SCALE * total_t + SIN_SCALE * total_s
        weighted = q * jnp.concatenate([basis] * 2, axis=0)
        real_z = jnp.sum(weighted[0:4], axis=0, keepdims=True)
        imag_z = jnp.sum(weighted[4:8], axis=0, keepdims=True)
        return [imag_z * (-wave_ref[f]), real_z * wave_ref[f]]

    first, second = (pl.ds(pl.multiple_of(i * width, width), width) for i in (step, steps + step))
    basis1 = basis_ref[0:4, first]
    basis2 = basis_ref[0:4, second]
    far1, far2 = [], []
    for f in range(FREQS):
        parts = masked_parts(parts_ref, f)
        for i in range(live_own // PIECE):
            at = slice(i * PIECE, (i + 1) * PIECE)
            turns = jnp.dot(y_ref[at, :], parts, preferred_element_type=F32)
            t_ref[steps + step, f, at, :], s_ref[steps + step, f, at, :] = half_angle(turns)
        total_t = jnp.dot(src_ref[f, 0], t_ref[steps + step, f], preferred_element_type=F32)
        total_s = jnp.dot(src_ref[f, 1], s_ref[steps + step, f], preferred_element_type=F32)
        far2 += project(f, total_t, total_s, basis2)
    for copy in fetch(step):
        copy.wait()
    for f in range(FREQS):
        total_t = jnp.dot(src_ref[f, 0], t_ref[step, f], preferred_element_type=F32)
        total_s = jnp.dot(src_ref[f, 1], s_ref[step, f], preferred_element_type=F32)
        far1 += project(f, total_t, total_s, basis1)
    far_ref[:, first] = jnp.concatenate(far1, axis=0)
    far_ref[:, second] = jnp.concatenate(far2, axis=0)


def adjoint_kernel(
    ends_ref, wave_ref, far_ref, target_ref, weight_ref, basis_ref, rows_ref,
    t_ref, s_ref, out_ref, cost_ref, _t, _s, flat_ref,
):
    live_own = rows_ref.shape[1]
    blocks = live_own // LANES
    count_dirs = far_ref.shape[1]
    width = t_ref.shape[3]
    mismatch = far_ref[...] - jnp.concatenate([target_ref[f] for f in range(FREQS)], axis=0)
    pull = weight_ref[...] * mismatch
    cost_ref[0] = jnp.sum(pull * mismatch) / count_dirs
    gradient = pull * (2.0 / count_dirs)
    basis = jnp.concatenate([basis_ref[0:4, :]] * 2, axis=0)
    contract = (((1,), (1,)), ((), ()))
    normal = rows_ref[3:6]
    pressure_real, pressure_imag, velocity_real, velocity_imag = [], [], [], []
    for f in range(FREQS):
        real_gz = jnp.broadcast_to(gradient[2 * f + 1 : 2 * f + 2] * wave_ref[f], (4, count_dirs))
        imag_gz = jnp.broadcast_to(gradient[2 * f : 2 * f + 1] * (-wave_ref[f]), (4, count_dirs))
        for_cos = (basis * jnp.concatenate([real_gz, imag_gz], axis=0)).astype(BF16)
        for_sin = (basis * jnp.concatenate([-imag_gz, real_gz], axis=0)).astype(BF16)
        whole = jnp.sum(for_cos.astype(F32), axis=1, keepdims=True)
        total_t = jnp.zeros((8, live_own), F32)
        total_s = jnp.zeros((8, live_own), F32)
        for i in range(t_ref.shape[0]):
            at = slice(i * width, (i + 1) * width)
            total_t += lax.dot_general(for_cos[:, at], t_ref[i, f], contract, preferred_element_type=F32)
            total_s += lax.dot_general(for_sin[:, at], s_ref[i, f], contract, preferred_element_type=F32)
        got = whole - COS_SCALE * total_t + SIN_SCALE * total_s
        pressure_real.append(jnp.sum(normal * got[1:4], axis=0, keepdims=True))
        pressure_imag.append(jnp.sum(normal * got[5:8], axis=0, keepdims=True))
        velocity_real.append(got[0:1])
        velocity_imag.append(got[4:5])
    flat = jnp.concatenate(pressure_real + pressure_imag + velocity_real + velocity_imag, axis=0)
    for b in range(blocks):
        flat_ref[b] = flat[:, b * LANES : (b + 1) * LANES]
    flat_ref[blocks] = jnp.zeros((16, LANES), F32)
    lane = lax.broadcasted_iota(jnp.int32, (16, LANES), 1)

    def body(s, carry):
        offset = ends_ref[0, s]
        base = offset // LANES
        shift = offset % LANES
        back = (LANES - shift) % LANES
        joined = jnp.where(lane >= shift, flat_ref[base], flat_ref[base + 1])
        joined = pltpu.roll(joined, back, 1)
        out_ref[s] = jnp.where(lane < ends_ref[1, s], joined, 0.0)
        return carry

    lax.fori_loop(0, out_ref.shape[0], body, 0, unroll=8)


def scatter_kernel(value_ref, index_ref, out_ref, *, chunk):
    tiles = value_ref.shape[0]
    high = out_ref.shape[1] // 256
    width = chunk * LANES
    contract = (((1,), (1,)), ((), ()))

    def body(step, total):
        base = step * chunk
        cell = jnp.concatenate([index_ref[base + t] for t in range(chunk)], axis=1)
        value = jnp.concatenate([value_ref[base + t] for t in range(chunk)], axis=1)
        hi = lax.shift_right_logical(cell, 8)
        lo = cell & 255
        level = lax.broadcasted_iota(jnp.int32, (256, width), 0)
        pick = jnp.where(level == lo, 1.0, 0.0).astype(BF16)
        value = value.astype(BF16)
        hi = jnp.broadcast_to(hi, (16, width)).astype(F32).astype(BF16)
        zero = jnp.zeros((16, width), BF16)
        spread = jnp.concatenate([jnp.where(hi == float(h), value, zero) for h in range(high)], axis=0)
        return total + lax.dot_general(spread, pick, contract, preferred_element_type=F32)

    total = jnp.zeros((high * 16, 256), F32)
    for step in range(tiles // chunk):
        total = body(step, total)
    for h in range(high):
        out_ref[:, h * 256 : (h + 1) * 256] = total[h * 16 : (h + 1) * 16, :]


def smem():
    return pl.BlockSpec(memory_space=pltpu.SMEM)


def params():
    return pltpu.CompilerParams(vmem_limit_bytes=VMEM_BYTES)


def to_tiles(x, cap):
    owners, channels, _ = x.shape
    if cap == LANES:
        return x
    many = LANES // cap
    x = x.reshape(owners // many, many, channels, cap).transpose(0, 2, 1, 3)
    return x.reshape(owners // many, channels, LANES)


def from_tiles(x, cap):
    tiles, channels, _ = x.shape
    if cap == LANES:
        return x
    many = LANES // cap
    x = x.reshape(tiles, channels, many, cap).transpose(0, 2, 1, 3)
    return x.reshape(tiles * many, channels, cap)


def all_sum(x):
    gx, gy = (lax.axis_size(axis) for axis in AXES)
    low = gy.bit_length() - 1
    rest = [b for b in range((gx * gy).bit_length() - 1) if b != low]
    rounds = [[low]]
    if low % 2:
        rounds.append([rest.pop(0), rest.pop(-1)])
    rounds += [rest[i : i + 2] for i in range(0, len(rest), 2)]
    for bits in rounds:
        masks = [sum(1 << b for k, b in enumerate(bits) if code >> k & 1) for code in range(1, 1 << len(bits))]
        came = [lax.ppermute(x, AXES, [(i, i ^ m) for i in range(gx * gy)]) for m in masks]
        if len(came) == 1:
            x = x + came[0]
        else:
            x = (x + came[0]) + (came[1] + came[2])
    return x


def on_device(cell_state, geometry, surface_cell, counts, wavenumbers, target, direction_weight):
    owners = lax.axis_size(AXES)
    rows_dev = surface_cell.shape[0]
    cells = cell_state.shape[1]
    cap = rows_dev // owners
    live_own = rows_dev // 4
    count_dirs = target.shape[2]
    tiles = rows_dev // LANES
    high = cells // 256
    basis, parts = direction_tables(count_dirs)
    basis, parts = jnp.asarray(basis), jnp.asarray(parts)
    vmem = pl.BlockSpec(memory_space=pltpu.VMEM)

    share = (counts // owners).astype(F32)
    rows = jnp.concatenate([geometry, jnp.broadcast_to(share[None, :], (1, rows_dev))], axis=0)
    rows = rows.reshape(8, cap, owners).transpose(2, 0, 1)
    came = lax.all_to_all(rows, AXES, split_axis=0, concat_axis=0, tiled=True)
    index = to_tiles(surface_cell.reshape(cap, owners).T.reshape(owners, 1, cap), cap)
    outgoing = pl.pallas_call(
        functools.partial(gather_kernel, chunk=4),
        in_specs=[vmem, vmem, vmem],
        out_shape=jax.ShapeDtypeStruct((tiles, 16, LANES), F32),
        scratch_shapes=[pltpu.VMEM((high * 16, 256), BF16), pltpu.VMEM((high * 16, 256), BF16)],
        compiler_params=params(),
        name="gather_rows",
    )(cell_state, index, to_tiles(rows, cap))
    values = lax.all_to_all(from_tiles(outgoing, cap), AXES, split_axis=0, concat_axis=0, tiled=True)
    marks = np.stack([np.tril(np.ones((owners, owners), np.float32), -1), np.eye(owners, dtype=np.float32)])
    ends = jnp.sum(came[:, 7, 0] * marks, axis=2).astype(jnp.int32)
    if cap < LANES:
        came = jnp.pad(came, ((0, 0), (0, 0), (0, LANES - cap)))
        values = jnp.pad(values, ((0, 0), (0, 0), (0, LANES - cap)))

    parts, basis, came, values = (pltpu.with_memory_space_constraint(x, pltpu.HBM) for x in (parts, basis, came, values))
    width = 256
    half = count_dirs // width // 2
    packs = live_own // LANES + 1
    first = pltpu.HBM((half, FREQS, live_own, width), BF16)
    held = pltpu.VMEM((2 * half, FREQS, live_own, width), BF16)
    block = pl.BlockSpec((1, FREQS, live_own, width), lambda i: (i, 0, 0, 0))
    first_t, first_s, kept, turned = pl.pallas_call(
        phase_kernel,
        grid=(half,),
        in_specs=[smem(), smem(), vmem, pl.BlockSpec((32 * FREQS, width), lambda i: (0, i))],
        out_specs=[block, block, vmem, vmem],
        out_shape=[
            first, first,
            pltpu.HBM((8, live_own), F32),
            pltpu.HBM((live_own, 32 * FREQS), BF16),
        ],
        scratch_shapes=[pltpu.VMEM((packs, 8, LANES), F32)],
        compiler_params=params(),
        name="phases",
    )(ends, wavenumbers, came, parts)

    hbm = pl.BlockSpec(memory_space=pltpu.HBM)
    far, t_all, s_all = pl.pallas_call(
        radiate_kernel,
        grid=(half,),
        in_specs=[
            smem(), smem(), vmem, vmem, vmem,
            pl.BlockSpec((32 * FREQS, width), lambda i: (0, half + i)),
            vmem, hbm, hbm,
        ],
        out_specs=[vmem] * 3,
        out_shape=[jax.ShapeDtypeStruct((2 * FREQS, count_dirs), F32), held, held],
        scratch_shapes=[
            pltpu.VMEM((packs, 16, LANES), F32),
            pltpu.VMEM((FREQS, 2, 8, live_own), BF16),
            pltpu.SemaphoreType.DMA((half,)),
            pltpu.SemaphoreType.DMA((half,)),
        ],
        compiler_params=params(),
        name="radiate",
    )(ends, wavenumbers, values, kept, turned, parts, basis, first_t, first_s)

    far = all_sum(far)

    back, objective = pl.pallas_call(
        adjoint_kernel,
        in_specs=[smem(), smem()] + [vmem] * 7,
        out_specs=[vmem, smem(), vmem, vmem],
        out_shape=[
            jax.ShapeDtypeStruct((owners, 16, LANES), F32),
            jax.ShapeDtypeStruct((1,), F32),
            held, held,
        ],
        input_output_aliases={7: 2, 8: 3},
        scratch_shapes=[pltpu.VMEM((packs, 16, LANES), F32)],
        compiler_params=params(),
        name="adjoint",
    )(
        ends, wavenumbers, far, target, direction_weight.reshape(1, count_dirs), basis, kept, t_all, s_all,
    )[:2]
    returned = lax.all_to_all(back[:, :, :cap], AXES, split_axis=0, concat_axis=0, tiled=True)
    cell_adjoint = pl.pallas_call(
        functools.partial(scatter_kernel, chunk=4),
        in_specs=[vmem, vmem],
        out_shape=jax.ShapeDtypeStruct(cell_state.shape, F32),
        compiler_params=params(),
        name="scatter_rows",
    )(to_tiles(returned, cap), index)
    return (far.reshape(FREQS, 2, count_dirs), objective[0], cell_adjoint)


def solution(mesh):
    placed = (
        P(None, AXES),
        P(None, AXES),
        P(AXES),
        P(AXES),
        P(),
        P(),
        P(),
    )
    return jax.shard_map(
        on_device,
        mesh=mesh,
        in_specs=placed,
        out_specs=(P(), P(), P(None, AXES)),
        check_vma=False,
    )
```

```python
import functools
import math

import jax
import jax.numpy as jnp
import numpy as np
from jax import lax
from jax.experimental import pallas as pl
from jax.experimental.pallas import tpu as pltpu
from jax.sharding import PartitionSpec as P

GOLDEN = math.pi * (3.0 - math.sqrt(5.0))
AXES = ("gx", "gy")
F32 = jnp.float32
BF16 = jnp.bfloat16
LANES = 128
FREQS = 4
VMEM_BYTES = 24 * 2**20
PIECE = 1024

SIN_K, SIN_A, SIN_B = 2.299546, 1.116939, 0.118212
COS_K, COS_A, COS_B = 3.583841, 0.682394, 0.186797
COS_SCALE = 2.0 * SIN_K * SIN_K
SIN_SCALE = 2.0 * SIN_K * COS_K


def direction_tables(count_dirs):
    lattice = np.arange(count_dirs).astype(np.float32)
    height = (np.float32(1.0) - (np.float32(2.0) * lattice + np.float32(1.0)) / np.float32(count_dirs)).astype(np.float32)
    radius_xy = np.sqrt(np.float32(1.0) - height * height).astype(np.float32)
    azimuth = np.mod(lattice * np.float32(GOLDEN), np.float32(2.0 * math.pi)).astype(np.float32)
    d = np.stack([radius_xy * np.cos(azimuth), radius_xy * np.sin(azimuth), height]).astype(np.float32)
    basis = np.concatenate([np.ones((1, count_dirs), np.float32), d, np.zeros((4, count_dirs), np.float32)])
    d1 = d.astype(jnp.bfloat16)
    d2 = (d - d1.astype(np.float32)).astype(jnp.bfloat16)
    d3 = (d - d1.astype(np.float32) - d2.astype(np.float32)).astype(jnp.bfloat16)
    parts = np.concatenate([d1, d1, d1, d2, d2, d3, d2, d3, np.zeros((8, count_dirs), d1.dtype)])
    return basis, np.concatenate([parts] * FREQS)


def bf16_parts(x):
    x1 = x.astype(BF16).astype(F32)
    x2 = (x - x1).astype(BF16).astype(F32)
    return x1, x2, x - x1 - x2


def gather_kernel(cell_ref, index_ref, rows_ref, out_ref, a1_ref, a2_ref, *, chunk):
    cells = cell_ref.shape[1]
    high = cells // 256
    for h in range(high):
        part = cell_ref[:, h * 256 : (h + 1) * 256]
        top = part.astype(BF16)
        a1_ref[h * 16 : (h + 1) * 16, :] = top
        a2_ref[h * 16 : (h + 1) * 16, :] = (part - top.astype(F32)).astype(BF16)
    tiles = out_ref.shape[0]

    for step in range(tiles // chunk):
        width = chunk * LANES
        base = step * chunk
        cell = jnp.concatenate([index_ref[base + t] for t in range(chunk)], axis=1)
        hi = lax.shift_right_logical(cell, 8)
        lo = cell & 255
        level = lax.broadcasted_iota(jnp.int32, (256, width), 0)
        pick = jnp.where(level == lo, 1.0, 0.0).astype(BF16)
        found = jnp.dot(a1_ref[...], pick, preferred_element_type=F32) + jnp.dot(
            a2_ref[...], pick, preferred_element_type=F32
        )
        hi = jnp.broadcast_to(hi, (16, width))
        total = jnp.zeros((16, width), F32)
        for h in range(high):
            total = jnp.where(hi == h, found[h * 16 : (h + 1) * 16, :], total)
        for t in range(chunk):
            out_ref[base + t] = total[:, t * LANES : (t + 1) * LANES] * rows_ref[base + t, 6:7, :]


def pack_rows(ends_ref, came_ref, packed_ref):
    sources, channels, _ = came_ref.shape
    lane = lax.broadcasted_iota(jnp.int32, (channels, LANES), 1)

    def body(s, carry):
        offset = ends_ref[0, s]
        base = offset // LANES
        shift = offset % LANES
        tile = pltpu.roll(came_ref[s], shift, 1)
        pltpu.store(packed_ref.at[base], tile, mask=lane >= shift)
        pltpu.store(packed_ref.at[base + 1], tile, mask=lane < shift)
        return carry

    lax.fori_loop(0, sources, body, 0, unroll=8)
    return jnp.concatenate([packed_ref[b] for b in range(packed_ref.shape[0] - 1)], axis=1)


def half_angle(turns):
    r = turns - jnp.round(turns)
    u = r * r
    v = u - SIN_A
    half_sin = (v * v + SIN_B) * r
    w = u - COS_A
    half_cos = w * w - COS_B
    return (half_sin * half_sin).astype(BF16), (half_sin * half_cos).astype(BF16)


def masked_parts(parts_ref, f):
    parts = parts_ref[...]
    level = lax.broadcasted_iota(jnp.int32, parts.shape, 0)
    return jnp.where((level >= 32 * f) & (level < 32 * f + 32), parts.astype(F32), 0.0).astype(BF16)


def phase_kernel(ends_ref, wave_ref, came_ref, parts_ref, t_ref, s_ref, rows_ref, y_ref, packed_ref):
    live_own = rows_ref.shape[1]

    @pl.when(pl.program_id(0) == 0)
    def _():
        rows = pack_rows(ends_ref, came_ref, packed_ref)
        rows_ref[...] = rows
        turned = []
        for f in range(FREQS):
            y1, y2, y3 = bf16_parts(rows[0:3] * (wave_ref[f] * (0.5 / math.pi)))
            turned += [y1, y2, y3, y1, y2, y1, y3, y2, jnp.zeros((8, live_own), F32)]
        y_ref[...] = jnp.concatenate(turned, axis=0).T.astype(BF16)

    for f in range(FREQS):
        parts = masked_parts(parts_ref, f)
        for i in range(live_own // PIECE):
            at = slice(i * PIECE, (i + 1) * PIECE)
            turns = jnp.dot(y_ref[at, :], parts, preferred_element_type=F32)
            t_ref[0, f, at, :], s_ref[0, f, at, :] = half_angle(turns)


def radiate_kernel(
    ends_ref, wave_ref, came_ref, rows_ref, y_ref, parts_ref, basis_ref, first_t_ref, first_s_ref,
    t_ref, s_ref, far_ref, packed_ref, src_ref, t_sem, s_sem,
):
    live_own = rows_ref.shape[1]
    step = pl.program_id(0)
    steps = pl.num_programs(0)
    half, _, _, width = first_t_ref.shape

    def fetch(i):
        return (
            pltpu.make_async_copy(first_t_ref.at[i], t_ref.at[i], t_sem.at[i]),
            pltpu.make_async_copy(first_s_ref.at[i], s_ref.at[i], s_sem.at[i]),
        )

    @pl.when(step == 0)
    def _():
        for i in range(half):
            for copy in fetch(i):
                copy.start()
        rows = pack_rows(ends_ref, came_ref, packed_ref)
        normal = rows_ref[3:6]
        for f in range(FREQS):
            real = jnp.concatenate([rows[8 + f : 9 + f], normal * rows[f : f + 1]], axis=0)
            imag = jnp.concatenate([rows[12 + f : 13 + f], normal * rows[4 + f : 5 + f]], axis=0)
            src_ref[f, 0] = jnp.concatenate([real, imag], axis=0).astype(BF16)
            src_ref[f, 1] = jnp.concatenate([imag, -real], axis=0).astype(BF16)

    def project(f, total_t, total_s, basis):
        whole = jnp.sum(src_ref[f, 0].astype(F32), axis=1, keepdims=True)
        q = whole - COS_SCALE * total_t + SIN_SCALE * total_s
        weighted = q * jnp.concatenate([basis] * 2, axis=0)
        real_z = jnp.sum(weighted[0:4], axis=0, keepdims=True)
        imag_z = jnp.sum(weighted[4:8], axis=0, keepdims=True)
        return [imag_z * (-wave_ref[f]), real_z * wave_ref[f]]

    first, second = (pl.ds(pl.multiple_of(i * width, width), width) for i in (step, steps + step))
    basis1 = basis_ref[0:4, first]
    basis2 = basis_ref[0:4, second]
    far1, far2 = [], []
    for f in range(FREQS):
        parts = masked_parts(parts_ref, f)
        for i in range(live_own // PIECE):
            at = slice(i * PIECE, (i + 1) * PIECE)
            turns = jnp.dot(y_ref[at, :], parts, preferred_element_type=F32)
            t_ref[steps + step, f, at, :], s_ref[steps + step, f, at, :] = half_angle(turns)
        total_t = jnp.dot(src_ref[f, 0], t_ref[steps + step, f], preferred_element_type=F32)
        total_s = jnp.dot(src_ref[f, 1], s_ref[steps + step, f], preferred_element_type=F32)
        far2 += project(f, total_t, total_s, basis2)
    for copy in fetch(step):
        copy.wait()
    for f in range(FREQS):
        total_t = jnp.dot(src_ref[f, 0], t_ref[step, f], preferred_element_type=F32)
        total_s = jnp.dot(src_ref[f, 1], s_ref[step, f], preferred_element_type=F32)
        far1 += project(f, total_t, total_s, basis1)
    far_ref[:, first] = jnp.concatenate(far1, axis=0)
    far_ref[:, second] = jnp.concatenate(far2, axis=0)


def adjoint_kernel(
    ends_ref, wave_ref, target_ref, weight_ref, basis_ref, rows_ref, t_ref, s_ref, *rest
):
    far_terms, (_t, _s, out_ref, cost_ref, far_ref, flat_ref) = rest[:-6], rest[-6:]
    far = far_terms[0][...]
    if len(far_terms) == 2:
        far = far + far_terms[1][...]
    else:
        far = (far + far_terms[1][...]) + (far_terms[2][...] + far_terms[3][...])
    for f in range(FREQS):
        far_ref[f] = far[2 * f : 2 * f + 2]

    live_own = rows_ref.shape[1]
    blocks = live_own // LANES
    count_dirs = far.shape[1]
    width = t_ref.shape[3]
    mismatch = far - jnp.concatenate([target_ref[f] for f in range(FREQS)], axis=0)
    pull = weight_ref[...] * mismatch
    cost_ref[0] = jnp.sum(pull * mismatch) / count_dirs
    gradient = pull * (2.0 / count_dirs)
    basis = jnp.concatenate([basis_ref[0:4, :]] * 2, axis=0)
    contract = (((1,), (1,)), ((), ()))
    normal = rows_ref[3:6]
    pressure_real, pressure_imag, velocity_real, velocity_imag = [], [], [], []
    for f in range(FREQS):
        real_gz = jnp.broadcast_to(gradient[2 * f + 1 : 2 * f + 2] * wave_ref[f], (4, count_dirs))
        imag_gz = jnp.broadcast_to(gradient[2 * f : 2 * f + 1] * (-wave_ref[f]), (4, count_dirs))
        for_cos = (basis * jnp.concatenate([real_gz, imag_gz], axis=0)).astype(BF16)
        for_sin = (basis * jnp.concatenate([-imag_gz, real_gz], axis=0)).astype(BF16)
        whole = jnp.sum(for_cos.astype(F32), axis=1, keepdims=True)
        total_t = jnp.zeros((8, live_own), F32)
        total_s = jnp.zeros((8, live_own), F32)
        for i in range(t_ref.shape[0]):
            at = slice(i * width, (i + 1) * width)
            total_t += lax.dot_general(for_cos[:, at], t_ref[i, f], contract, preferred_element_type=F32)
            total_s += lax.dot_general(for_sin[:, at], s_ref[i, f], contract, preferred_element_type=F32)
        got = whole - COS_SCALE * total_t + SIN_SCALE * total_s
        pressure_real.append(jnp.sum(normal * got[1:4], axis=0, keepdims=True))
        pressure_imag.append(jnp.sum(normal * got[5:8], axis=0, keepdims=True))
        velocity_real.append(got[0:1])
        velocity_imag.append(got[4:5])
    flat = jnp.concatenate(pressure_real + pressure_imag + velocity_real + velocity_imag, axis=0)
    for b in range(blocks):
        flat_ref[b] = flat[:, b * LANES : (b + 1) * LANES]
    flat_ref[blocks] = jnp.zeros((16, LANES), F32)
    lane = lax.broadcasted_iota(jnp.int32, (16, LANES), 1)

    def body(s, carry):
        offset = ends_ref[0, s]
        base = offset // LANES
        shift = offset % LANES
        back = (LANES - shift) % LANES
        joined = jnp.where(lane >= shift, flat_ref[base], flat_ref[base + 1])
        joined = pltpu.roll(joined, back, 1)
        out_ref[s] = jnp.where(lane < ends_ref[1, s], joined, 0.0)
        return carry

    lax.fori_loop(0, out_ref.shape[0], body, 0, unroll=8)


def scatter_kernel(value_ref, index_ref, out_ref, *, chunk):
    tiles = value_ref.shape[0]
    high = out_ref.shape[1] // 256
    width = chunk * LANES
    contract = (((1,), (1,)), ((), ()))

    def body(step, total):
        base = step * chunk
        cell = jnp.concatenate([index_ref[base + t] for t in range(chunk)], axis=1)
        value = jnp.concatenate([value_ref[base + t] for t in range(chunk)], axis=1)
        hi = lax.shift_right_logical(cell, 8)
        lo = cell & 255
        level = lax.broadcasted_iota(jnp.int32, (256, width), 0)
        pick = jnp.where(level == lo, 1.0, 0.0).astype(BF16)
        value = value.astype(BF16)
        hi = jnp.broadcast_to(hi, (16, width)).astype(F32).astype(BF16)
        zero = jnp.zeros((16, width), BF16)
        spread = jnp.concatenate([jnp.where(hi == float(h), value, zero) for h in range(high)], axis=0)
        return total + lax.dot_general(spread, pick, contract, preferred_element_type=F32)

    total = jnp.zeros((high * 16, 256), F32)
    for step in range(tiles // chunk):
        total = body(step, total)
    for h in range(high):
        out_ref[:, h * 256 : (h + 1) * 256] = total[h * 16 : (h + 1) * 16, :]


def smem():
    return pl.BlockSpec(memory_space=pltpu.SMEM)


def params():
    return pltpu.CompilerParams(vmem_limit_bytes=VMEM_BYTES)


def to_tiles(x, cap):
    owners, channels, _ = x.shape
    if cap == LANES:
        return x
    many = LANES // cap
    x = x.reshape(owners // many, many, channels, cap).transpose(0, 2, 1, 3)
    return x.reshape(owners // many, channels, LANES)


def from_tiles(x, cap):
    tiles, channels, _ = x.shape
    if cap == LANES:
        return x
    many = LANES // cap
    x = x.reshape(tiles, channels, many, cap).transpose(0, 2, 1, 3)
    return x.reshape(tiles * many, channels, cap)


def all_sum(x):
    gx, gy = (lax.axis_size(axis) for axis in AXES)
    low = gy.bit_length() - 1
    rest = [b for b in range((gx * gy).bit_length() - 1) if b != low]
    rounds = [[low]]
    if low % 2:
        rounds.append([rest.pop(0), rest.pop(-1)])
    rounds += [rest[i : i + 2] for i in range(0, len(rest), 2)]
    for bits in rounds:
        masks = [sum(1 << b for k, b in enumerate(bits) if code >> k & 1) for code in range(1, 1 << len(bits))]
        came = [lax.ppermute(x, AXES, [(i, i ^ m) for i in range(gx * gy)]) for m in masks]
        if bits is rounds[-1]:
            return [x] + came
        x = x + came[0] if len(came) == 1 else (x + came[0]) + (came[1] + came[2])


def on_device(cell_state, geometry, surface_cell, counts, wavenumbers, target, direction_weight):
    owners = lax.axis_size(AXES)
    rows_dev = surface_cell.shape[0]
    cells = cell_state.shape[1]
    cap = rows_dev // owners
    live_own = rows_dev // 4
    count_dirs = target.shape[2]
    tiles = rows_dev // LANES
    high = cells // 256
    basis, parts = direction_tables(count_dirs)
    basis, parts, wavenumbers, cell_state = (
        pltpu.with_memory_space_constraint(x, pltpu.HBM)
        for x in (jnp.asarray(basis), jnp.asarray(parts), wavenumbers, cell_state)
    )
    vmem = pl.BlockSpec(memory_space=pltpu.VMEM)

    share = (counts // owners).astype(F32)
    rows = jnp.concatenate([geometry, jnp.broadcast_to(share[None, :], (1, rows_dev))], axis=0)
    rows = rows.reshape(8, cap, owners).transpose(2, 0, 1)
    came = lax.all_to_all(rows, AXES, split_axis=0, concat_axis=0, tiled=True)
    index = to_tiles(surface_cell.reshape(cap, owners).T.reshape(owners, 1, cap), cap)
    outgoing = pl.pallas_call(
        functools.partial(gather_kernel, chunk=4),
        in_specs=[vmem, vmem, vmem],
        out_shape=jax.ShapeDtypeStruct((tiles, 16, LANES), F32),
        scratch_shapes=[pltpu.VMEM((high * 16, 256), BF16), pltpu.VMEM((high * 16, 256), BF16)],
        compiler_params=params(),
        name="gather_rows",
    )(cell_state, index, to_tiles(rows, cap))
    values = lax.all_to_all(from_tiles(outgoing, cap), AXES, split_axis=0, concat_axis=0, tiled=True)
    me, other = jnp.arange(2 * owners)[:, None], jnp.arange(owners)[None, :]
    counted = jnp.where(me < owners, other < me, other == me - owners)
    ends = jnp.sum(jnp.where(counted, came[:, 7, 0][None, :], 0.0), axis=1).astype(jnp.int32).reshape(2, owners)
    if cap < LANES:
        came = jnp.pad(came, ((0, 0), (0, 0), (0, LANES - cap)))
        values = jnp.pad(values, ((0, 0), (0, 0), (0, LANES - cap)))

    width = 256
    half = count_dirs // width // 2
    packs = live_own // LANES + 1
    first = pltpu.HBM((half, FREQS, live_own, width), BF16)
    held = pltpu.VMEM((2 * half, FREQS, live_own, width), BF16)
    block = pl.BlockSpec((1, FREQS, live_own, width), lambda i: (i, 0, 0, 0))
    first_t, first_s, kept, turned = pl.pallas_call(
        phase_kernel,
        grid=(half,),
        in_specs=[smem(), smem(), vmem, pl.BlockSpec((32 * FREQS, width), lambda i: (0, i))],
        out_specs=[block, block, vmem, vmem],
        out_shape=[
            first, first,
            pltpu.HBM((8, live_own), F32),
            pltpu.HBM((live_own, 32 * FREQS), BF16),
        ],
        scratch_shapes=[pltpu.VMEM((packs, 8, LANES), F32)],
        compiler_params=params(),
        name="phases",
    )(ends, wavenumbers, came, parts)

    hbm = pl.BlockSpec(memory_space=pltpu.HBM)
    t_all, s_all, far = pl.pallas_call(
        radiate_kernel,
        grid=(half,),
        in_specs=[
            smem(), smem(), vmem, vmem, vmem,
            pl.BlockSpec((32 * FREQS, width), lambda i: (0, half + i)),
            vmem, hbm, hbm,
        ],
        out_specs=[vmem] * 3,
        out_shape=[held, held, pltpu.VMEM((2 * FREQS, count_dirs), F32)],
        scratch_shapes=[
            pltpu.VMEM((packs, 16, LANES), F32),
            pltpu.VMEM((FREQS, 2, 8, live_own), BF16),
            pltpu.SemaphoreType.DMA((half,)),
            pltpu.SemaphoreType.DMA((half,)),
        ],
        compiler_params=params(),
        name="radiate",
    )(ends, wavenumbers, values, kept, turned, parts, basis, first_t, first_s)

    far_terms = [pltpu.with_memory_space_constraint(x, pltpu.VMEM) for x in all_sum(far)]

    _, _, back, objective, far = pl.pallas_call(
        adjoint_kernel,
        in_specs=[smem(), smem()] + [vmem] * (6 + len(far_terms)),
        out_specs=[vmem, vmem, vmem, smem(), vmem],
        out_shape=[
            held, held,
            jax.ShapeDtypeStruct((owners, 16, LANES), F32),
            jax.ShapeDtypeStruct((1,), F32),
            jax.ShapeDtypeStruct(target.shape, F32),
        ],
        input_output_aliases={6: 0, 7: 1},
        scratch_shapes=[pltpu.VMEM((packs, 16, LANES), F32)],
        compiler_params=params(),
        name="adjoint",
    )(
        ends, wavenumbers, target, direction_weight.reshape(1, count_dirs), basis, kept, t_all, s_all, *far_terms,
    )
    returned = lax.all_to_all(back[:, :, :cap], AXES, split_axis=0, concat_axis=0, tiled=True)
    cell_adjoint = pl.pallas_call(
        functools.partial(scatter_kernel, chunk=4),
        in_specs=[vmem, vmem],
        out_shape=jax.ShapeDtypeStruct(cell_state.shape, F32),
        compiler_params=params(),
        name="scatter_rows",
    )(to_tiles(returned, cap), index)
    return (far, objective[0], cell_adjoint)


def solution(mesh):
    placed = (
        P(None, AXES),
        P(None, AXES),
        P(AXES),
        P(AXES),
        P(),
        P(),
        P(),
    )
    return jax.shard_map(
        on_device,
        mesh=mesh,
        in_specs=placed,
        out_specs=(P(), P(), P(None, AXES)),
        check_vma=False,
    )
```

```python
import functools
import math

import jax
import jax.numpy as jnp
import numpy as np
from jax import lax
from jax.experimental import pallas as pl
from jax.experimental.pallas import tpu as pltpu
from jax.sharding import PartitionSpec as P

GOLDEN = math.pi * (3.0 - math.sqrt(5.0))
AXES = ("gx", "gy")
F32 = jnp.float32
BF16 = jnp.bfloat16
LANES = 128
FREQS = 4
VMEM_BYTES = 24 * 2**20
PIECE = 1024

SIN_K, SIN_A, SIN_B = 2.299546, 1.116939, 0.118212
COS_K, COS_A, COS_B = 3.583841, 0.682394, 0.186797
COS_SCALE = 2.0 * SIN_K * SIN_K
SIN_SCALE = 2.0 * SIN_K * COS_K


def direction_tables(count_dirs):
    lattice = np.arange(count_dirs).astype(np.float32)
    height = (np.float32(1.0) - (np.float32(2.0) * lattice + np.float32(1.0)) / np.float32(count_dirs)).astype(np.float32)
    radius_xy = np.sqrt(np.float32(1.0) - height * height).astype(np.float32)
    azimuth = np.mod(lattice * np.float32(GOLDEN), np.float32(2.0 * math.pi)).astype(np.float32)
    d = np.stack([radius_xy * np.cos(azimuth), radius_xy * np.sin(azimuth), height]).astype(np.float32)
    basis = np.concatenate([np.ones((1, count_dirs), np.float32), d, np.zeros((4, count_dirs), np.float32)])
    d1 = d.astype(jnp.bfloat16)
    d2 = (d - d1.astype(np.float32)).astype(jnp.bfloat16)
    d3 = (d - d1.astype(np.float32) - d2.astype(np.float32)).astype(jnp.bfloat16)
    parts = np.concatenate([d1, d1, d1, d2, d2, d3, d2, d3, np.zeros((8, count_dirs), d1.dtype)])
    return basis, np.concatenate([parts] * FREQS)


def bf16_parts(x):
    x1 = x.astype(BF16).astype(F32)
    x2 = (x - x1).astype(BF16).astype(F32)
    return x1, x2, x - x1 - x2


def gather_kernel(cell_ref, index_ref, rows_ref, out_ref, a1_ref, a2_ref, *, chunk):
    cells = cell_ref.shape[1]
    high = cells // 256
    for h in range(high):
        part = cell_ref[:, h * 256 : (h + 1) * 256]
        top = part.astype(BF16)
        a1_ref[h * 16 : (h + 1) * 16, :] = top
        a2_ref[h * 16 : (h + 1) * 16, :] = (part - top.astype(F32)).astype(BF16)
    tiles = out_ref.shape[0]

    for step in range(tiles // chunk):
        width = chunk * LANES
        base = step * chunk
        cell = jnp.concatenate([index_ref[base + t] for t in range(chunk)], axis=1)
        hi = lax.shift_right_logical(cell, 8)
        lo = cell & 255
        level = lax.broadcasted_iota(jnp.int32, (256, width), 0)
        pick = jnp.where(level == lo, 1.0, 0.0).astype(BF16)
        found = jnp.dot(a1_ref[...], pick, preferred_element_type=F32) + jnp.dot(
            a2_ref[...], pick, preferred_element_type=F32
        )
        hi = jnp.broadcast_to(hi, (16, width))
        total = jnp.zeros((16, width), F32)
        for h in range(high):
            total = jnp.where(hi == h, found[h * 16 : (h + 1) * 16, :], total)
        for t in range(chunk):
            out_ref[base + t] = total[:, t * LANES : (t + 1) * LANES] * rows_ref[base + t, 6:7, :]


def pack_rows(ends_ref, came_ref, packed_ref):
    sources, channels, _ = came_ref.shape
    lane = lax.broadcasted_iota(jnp.int32, (channels, LANES), 1)

    def body(s, carry):
        offset = ends_ref[0, s]
        base = offset // LANES
        shift = offset % LANES
        tile = pltpu.roll(came_ref[s], shift, 1)
        pltpu.store(packed_ref.at[base], tile, mask=lane >= shift)
        pltpu.store(packed_ref.at[base + 1], tile, mask=lane < shift)
        return carry

    lax.fori_loop(0, sources, body, 0, unroll=8)
    return jnp.concatenate([packed_ref[b] for b in range(packed_ref.shape[0] - 1)], axis=1)


def half_angle(turns):
    r = turns - jnp.round(turns)
    u = r * r
    v = u - SIN_A
    half_sin = ((v * v + SIN_B) * r).astype(BF16)
    w = u - COS_A
    half_cos = (w * w - COS_B).astype(BF16)
    return half_sin * half_sin, half_sin * half_cos


def masked_parts(parts_ref, f):
    parts = parts_ref[...]
    level = lax.broadcasted_iota(jnp.int32, parts.shape, 0)
    return jnp.where((level >= 32 * f) & (level < 32 * f + 32), parts.astype(F32), 0.0).astype(BF16)


def phase_kernel(ends_ref, wave_ref, came_ref, parts_ref, t_ref, s_ref, rows_ref, y_ref, packed_ref):
    live_own = rows_ref.shape[1]

    @pl.when(pl.program_id(0) == 0)
    def _():
        rows = pack_rows(ends_ref, came_ref, packed_ref)
        rows_ref[...] = rows
        turned = []
        for f in range(FREQS):
            y1, y2, y3 = bf16_parts(rows[0:3] * (wave_ref[f] * (0.5 / math.pi)))
            turned += [y1, y2, y3, y1, y2, y1, y3, y2, jnp.zeros((8, live_own), F32)]
        y_ref[...] = jnp.concatenate(turned, axis=0).T.astype(BF16)

    for f in range(FREQS):
        parts = masked_parts(parts_ref, f)
        for i in range(live_own // PIECE):
            at = slice(i * PIECE, (i + 1) * PIECE)
            turns = jnp.dot(y_ref[at, :], parts, preferred_element_type=F32)
            t_ref[0, f, at, :], s_ref[0, f, at, :] = half_angle(turns)


def radiate_kernel(
    ends_ref, wave_ref, came_ref, rows_ref, y_ref, parts_ref, basis_ref, first_t_ref, first_s_ref,
    t_ref, s_ref, far_ref, packed_ref, src_ref, t_sem, s_sem,
):
    live_own = rows_ref.shape[1]
    step = pl.program_id(0)
    steps = pl.num_programs(0)
    half, _, _, width = first_t_ref.shape

    def fetch(i):
        return (
            pltpu.make_async_copy(first_t_ref.at[i], t_ref.at[i], t_sem.at[i]),
            pltpu.make_async_copy(first_s_ref.at[i], s_ref.at[i], s_sem.at[i]),
        )

    @pl.when(step == 0)
    def _():
        for i in range(half):
            for copy in fetch(i):
                copy.start()
        rows = pack_rows(ends_ref, came_ref, packed_ref)
        normal = rows_ref[3:6]
        for f in range(FREQS):
            real = jnp.concatenate([rows[8 + f : 9 + f], normal * rows[f : f + 1]], axis=0)
            imag = jnp.concatenate([rows[12 + f : 13 + f], normal * rows[4 + f : 5 + f]], axis=0)
            src_ref[f, 0] = jnp.concatenate([real, imag], axis=0).astype(BF16)
            src_ref[f, 1] = jnp.concatenate([imag, -real], axis=0).astype(BF16)

    def project(f, total_t, total_s, basis):
        whole = jnp.sum(src_ref[f, 0].astype(F32), axis=1, keepdims=True)
        q = whole - COS_SCALE * total_t + SIN_SCALE * total_s
        weighted = q * jnp.concatenate([basis] * 2, axis=0)
        real_z = jnp.sum(weighted[0:4], axis=0, keepdims=True)
        imag_z = jnp.sum(weighted[4:8], axis=0, keepdims=True)
        return [imag_z * (-wave_ref[f]), real_z * wave_ref[f]]

    first, second = (pl.ds(pl.multiple_of(i * width, width), width) for i in (step, steps + step))
    basis1 = basis_ref[0:4, first]
    basis2 = basis_ref[0:4, second]
    far1, far2 = [], []
    for f in range(FREQS):
        parts = masked_parts(parts_ref, f)
        for i in range(live_own // PIECE):
            at = slice(i * PIECE, (i + 1) * PIECE)
            turns = jnp.dot(y_ref[at, :], parts, preferred_element_type=F32)
            t_ref[steps + step, f, at, :], s_ref[steps + step, f, at, :] = half_angle(turns)
        total_t = jnp.dot(src_ref[f, 0], t_ref[steps + step, f], preferred_element_type=F32)
        total_s = jnp.dot(src_ref[f, 1], s_ref[steps + step, f], preferred_element_type=F32)
        far2 += project(f, total_t, total_s, basis2)
    for copy in fetch(step):
        copy.wait()
    for f in range(FREQS):
        total_t = jnp.dot(src_ref[f, 0], t_ref[step, f], preferred_element_type=F32)
        total_s = jnp.dot(src_ref[f, 1], s_ref[step, f], preferred_element_type=F32)
        far1 += project(f, total_t, total_s, basis1)
    far_ref[:, first] = jnp.concatenate(far1, axis=0)
    far_ref[:, second] = jnp.concatenate(far2, axis=0)


def adjoint_kernel(
    ends_ref, wave_ref, target_ref, weight_ref, basis_ref, rows_ref, t_ref, s_ref, *rest
):
    far_terms, (_t, _s, out_ref, cost_ref, far_ref, flat_ref) = rest[:-6], rest[-6:]
    far = far_terms[0][...]
    if len(far_terms) == 2:
        far = far + far_terms[1][...]
    else:
        far = (far + far_terms[1][...]) + (far_terms[2][...] + far_terms[3][...])
    for f in range(FREQS):
        far_ref[f] = far[2 * f : 2 * f + 2]

    live_own = rows_ref.shape[1]
    blocks = live_own // LANES
    count_dirs = far.shape[1]
    width = t_ref.shape[3]
    mismatch = far - jnp.concatenate([target_ref[f] for f in range(FREQS)], axis=0)
    pull = weight_ref[...] * mismatch
    cost_ref[0] = jnp.sum(pull * mismatch) / count_dirs
    gradient = pull * (2.0 / count_dirs)
    basis = jnp.concatenate([basis_ref[0:4, :]] * 2, axis=0)
    contract = (((1,), (1,)), ((), ()))
    normal = rows_ref[3:6]
    pressure_real, pressure_imag, velocity_real, velocity_imag = [], [], [], []
    for f in range(FREQS):
        real_gz = jnp.broadcast_to(gradient[2 * f + 1 : 2 * f + 2] * wave_ref[f], (4, count_dirs))
        imag_gz = jnp.broadcast_to(gradient[2 * f : 2 * f + 1] * (-wave_ref[f]), (4, count_dirs))
        for_cos = (basis * jnp.concatenate([real_gz, imag_gz], axis=0)).astype(BF16)
        for_sin = (basis * jnp.concatenate([-imag_gz, real_gz], axis=0)).astype(BF16)
        whole = jnp.sum(for_cos.astype(F32), axis=1, keepdims=True)
        total_t = jnp.zeros((8, live_own), F32)
        total_s = jnp.zeros((8, live_own), F32)
        for i in range(t_ref.shape[0]):
            at = slice(i * width, (i + 1) * width)
            total_t += lax.dot_general(for_cos[:, at], t_ref[i, f], contract, preferred_element_type=F32)
            total_s += lax.dot_general(for_sin[:, at], s_ref[i, f], contract, preferred_element_type=F32)
        got = whole - COS_SCALE * total_t + SIN_SCALE * total_s
        pressure_real.append(jnp.sum(normal * got[1:4], axis=0, keepdims=True))
        pressure_imag.append(jnp.sum(normal * got[5:8], axis=0, keepdims=True))
        velocity_real.append(got[0:1])
        velocity_imag.append(got[4:5])
    flat = jnp.concatenate(pressure_real + pressure_imag + velocity_real + velocity_imag, axis=0)
    for b in range(blocks):
        flat_ref[b] = flat[:, b * LANES : (b + 1) * LANES]
    flat_ref[blocks] = jnp.zeros((16, LANES), F32)
    lane = lax.broadcasted_iota(jnp.int32, (16, LANES), 1)

    def body(s, carry):
        offset = ends_ref[0, s]
        base = offset // LANES
        shift = offset % LANES
        back = (LANES - shift) % LANES
        joined = jnp.where(lane >= shift, flat_ref[base], flat_ref[base + 1])
        joined = pltpu.roll(joined, back, 1)
        out_ref[s] = jnp.where(lane < ends_ref[1, s], joined, 0.0)
        return carry

    lax.fori_loop(0, out_ref.shape[0], body, 0, unroll=8)


def scatter_kernel(value_ref, index_ref, out_ref, *, chunk):
    tiles = value_ref.shape[0]
    high = out_ref.shape[1] // 256
    width = chunk * LANES
    contract = (((1,), (1,)), ((), ()))

    def body(step, total):
        base = step * chunk
        cell = jnp.concatenate([index_ref[base + t] for t in range(chunk)], axis=1)
        value = jnp.concatenate([value_ref[base + t] for t in range(chunk)], axis=1)
        hi = lax.shift_right_logical(cell, 8)
        lo = cell & 255
        level = lax.broadcasted_iota(jnp.int32, (256, width), 0)
        pick = jnp.where(level == lo, 1.0, 0.0).astype(BF16)
        value = value.astype(BF16)
        hi = jnp.broadcast_to(hi, (16, width)).astype(F32).astype(BF16)
        zero = jnp.zeros((16, width), BF16)
        spread = jnp.concatenate([jnp.where(hi == float(h), value, zero) for h in range(high)], axis=0)
        return total + lax.dot_general(spread, pick, contract, preferred_element_type=F32)

    total = jnp.zeros((high * 16, 256), F32)
    for step in range(tiles // chunk):
        total = body(step, total)
    for h in range(high):
        out_ref[:, h * 256 : (h + 1) * 256] = total[h * 16 : (h + 1) * 16, :]


def smem():
    return pl.BlockSpec(memory_space=pltpu.SMEM)


def params():
    return pltpu.CompilerParams(vmem_limit_bytes=VMEM_BYTES)


def to_tiles(x, cap):
    owners, channels, _ = x.shape
    if cap == LANES:
        return x
    many = LANES // cap
    x = x.reshape(owners // many, many, channels, cap).transpose(0, 2, 1, 3)
    return x.reshape(owners // many, channels, LANES)


def from_tiles(x, cap):
    tiles, channels, _ = x.shape
    if cap == LANES:
        return x
    many = LANES // cap
    x = x.reshape(tiles, channels, many, cap).transpose(0, 2, 1, 3)
    return x.reshape(tiles * many, channels, cap)


def all_sum(x):
    gx, gy = (lax.axis_size(axis) for axis in AXES)
    low = gy.bit_length() - 1
    rest = [b for b in range((gx * gy).bit_length() - 1) if b != low]
    rounds = [[low]]
    if low % 2:
        rounds.append([rest.pop(0), rest.pop(-1)])
    rounds += [rest[i : i + 2] for i in range(0, len(rest), 2)]
    for bits in rounds:
        masks = [sum(1 << b for k, b in enumerate(bits) if code >> k & 1) for code in range(1, 1 << len(bits))]
        came = [lax.ppermute(x, AXES, [(i, i ^ m) for i in range(gx * gy)]) for m in masks]
        if bits is rounds[-1]:
            return [x] + came
        x = x + came[0] if len(came) == 1 else (x + came[0]) + (came[1] + came[2])


def on_device(cell_state, geometry, surface_cell, counts, wavenumbers, target, direction_weight):
    owners = lax.axis_size(AXES)
    rows_dev = surface_cell.shape[0]
    cells = cell_state.shape[1]
    cap = rows_dev // owners
    live_own = rows_dev // 4
    count_dirs = target.shape[2]
    tiles = rows_dev // LANES
    high = cells // 256
    basis, parts = direction_tables(count_dirs)
    basis, parts, wavenumbers, cell_state = (
        pltpu.with_memory_space_constraint(x, pltpu.HBM)
        for x in (jnp.asarray(basis), jnp.asarray(parts), wavenumbers, cell_state)
    )
    vmem = pl.BlockSpec(memory_space=pltpu.VMEM)

    share = (counts // owners).astype(F32)
    rows = jnp.concatenate([geometry, jnp.broadcast_to(share[None, :], (1, rows_dev))], axis=0)
    rows = rows.reshape(8, cap, owners).transpose(2, 0, 1)
    came = lax.all_to_all(rows, AXES, split_axis=0, concat_axis=0, tiled=True)
    index = to_tiles(surface_cell.reshape(cap, owners).T.reshape(owners, 1, cap), cap)
    outgoing = pl.pallas_call(
        functools.partial(gather_kernel, chunk=4),
        in_specs=[vmem, vmem, vmem],
        out_shape=jax.ShapeDtypeStruct((tiles, 16, LANES), F32),
        scratch_shapes=[pltpu.VMEM((high * 16, 256), BF16), pltpu.VMEM((high * 16, 256), BF16)],
        compiler_params=params(),
        name="gather_rows",
    )(cell_state, index, to_tiles(rows, cap))
    values = lax.all_to_all(from_tiles(outgoing, cap), AXES, split_axis=0, concat_axis=0, tiled=True)
    me, other = jnp.arange(2 * owners)[:, None], jnp.arange(owners)[None, :]
    counted = jnp.where(me < owners, other < me, other == me - owners)
    ends = jnp.sum(jnp.where(counted, came[:, 7, 0][None, :], 0.0), axis=1).astype(jnp.int32).reshape(2, owners)
    if cap < LANES:
        came = jnp.pad(came, ((0, 0), (0, 0), (0, LANES - cap)))
        values = jnp.pad(values, ((0, 0), (0, 0), (0, LANES - cap)))

    width = 256
    half = count_dirs // width // 2
    packs = live_own // LANES + 1
    first = pltpu.HBM((half, FREQS, live_own, width), BF16)
    held = pltpu.VMEM((2 * half, FREQS, live_own, width), BF16)
    block = pl.BlockSpec((1, FREQS, live_own, width), lambda i: (i, 0, 0, 0))
    first_t, first_s, kept, turned = pl.pallas_call(
        phase_kernel,
        grid=(half,),
        in_specs=[smem(), smem(), vmem, pl.BlockSpec((32 * FREQS, width), lambda i: (0, i))],
        out_specs=[block, block, vmem, vmem],
        out_shape=[
            first, first,
            pltpu.HBM((8, live_own), F32),
            pltpu.HBM((live_own, 32 * FREQS), BF16),
        ],
        scratch_shapes=[pltpu.VMEM((packs, 8, LANES), F32)],
        compiler_params=params(),
        name="phases",
    )(ends, wavenumbers, came, parts)

    hbm = pl.BlockSpec(memory_space=pltpu.HBM)
    t_all, s_all, far = pl.pallas_call(
        radiate_kernel,
        grid=(half,),
        in_specs=[
            smem(), smem(), vmem, vmem, vmem,
            pl.BlockSpec((32 * FREQS, width), lambda i: (0, half + i)),
            vmem, hbm, hbm,
        ],
        out_specs=[vmem] * 3,
        out_shape=[held, held, pltpu.VMEM((2 * FREQS, count_dirs), F32)],
        scratch_shapes=[
            pltpu.VMEM((packs, 16, LANES), F32),
            pltpu.VMEM((FREQS, 2, 8, live_own), BF16),
            pltpu.SemaphoreType.DMA((half,)),
            pltpu.SemaphoreType.DMA((half,)),
        ],
        compiler_params=params(),
        name="radiate",
    )(ends, wavenumbers, values, kept, turned, parts, basis, first_t, first_s)

    far_terms = [pltpu.with_memory_space_constraint(x, pltpu.VMEM) for x in all_sum(far)]

    _, _, back, objective, far = pl.pallas_call(
        adjoint_kernel,
        in_specs=[smem(), smem()] + [vmem] * (6 + len(far_terms)),
        out_specs=[vmem, vmem, vmem, smem(), vmem],
        out_shape=[
            held, held,
            jax.ShapeDtypeStruct((owners, 16, LANES), F32),
            jax.ShapeDtypeStruct((1,), F32),
            jax.ShapeDtypeStruct(target.shape, F32),
        ],
        input_output_aliases={6: 0, 7: 1},
        scratch_shapes=[pltpu.VMEM((packs, 16, LANES), F32)],
        compiler_params=params(),
        name="adjoint",
    )(
        ends, wavenumbers, target, direction_weight.reshape(1, count_dirs), basis, kept, t_all, s_all, *far_terms,
    )
    returned = lax.all_to_all(back[:, :, :cap], AXES, split_axis=0, concat_axis=0, tiled=True)
    cell_adjoint = pl.pallas_call(
        functools.partial(scatter_kernel, chunk=4),
        in_specs=[vmem, vmem],
        out_shape=jax.ShapeDtypeStruct(cell_state.shape, F32),
        compiler_params=params(),
        name="scatter_rows",
    )(to_tiles(returned, cap), index)
    return (far, objective[0], cell_adjoint)


def solution(mesh):
    placed = (
        P(None, AXES),
        P(None, AXES),
        P(AXES),
        P(AXES),
        P(),
        P(),
        P(),
    )
    return jax.shard_map(
        on_device,
        mesh=mesh,
        in_specs=placed,
        out_specs=(P(), P(), P(None, AXES)),
        check_vma=False,
    )
```

```python
import functools
import math

import jax
import jax.numpy as jnp
import numpy as np
from jax import lax
from jax.experimental import pallas as pl
from jax.experimental.pallas import tpu as pltpu
from jax.sharding import PartitionSpec as P

GOLDEN = math.pi * (3.0 - math.sqrt(5.0))
AXES = ("gx", "gy")
F32 = jnp.float32
BF16 = jnp.bfloat16
LANES = 128
FREQS = 4
VMEM_BYTES = 24 * 2**20
PIECE = 1024

SIN_K, SIN_A, SIN_B = 2.299546, 1.116939, 0.118212
COS_K, COS_A, COS_B = 3.583841, 0.682394, 0.186797
COS_SCALE = 2.0 * SIN_K * SIN_K
SIN_SCALE = 2.0 * SIN_K * COS_K


def direction_tables(count_dirs):
    lattice = np.arange(count_dirs).astype(np.float32)
    height = (np.float32(1.0) - (np.float32(2.0) * lattice + np.float32(1.0)) / np.float32(count_dirs)).astype(np.float32)
    radius_xy = np.sqrt(np.float32(1.0) - height * height).astype(np.float32)
    azimuth = np.mod(lattice * np.float32(GOLDEN), np.float32(2.0 * math.pi)).astype(np.float32)
    d = np.stack([radius_xy * np.cos(azimuth), radius_xy * np.sin(azimuth), height]).astype(np.float32)
    basis = np.concatenate([np.ones((1, count_dirs), np.float32), d, np.zeros((4, count_dirs), np.float32)])
    d1 = d.astype(jnp.bfloat16)
    d2 = (d - d1.astype(np.float32)).astype(jnp.bfloat16)
    d3 = (d - d1.astype(np.float32) - d2.astype(np.float32)).astype(jnp.bfloat16)
    parts = np.concatenate([d1, d1, d1, d2, d2, d3, d2, d3, np.zeros((8, count_dirs), d1.dtype)])
    return basis, np.concatenate([parts] * FREQS)


def bf16_parts(x):
    x1 = x.astype(BF16).astype(F32)
    x2 = (x - x1).astype(BF16).astype(F32)
    return x1, x2, x - x1 - x2


def gather_kernel(cell_ref, index_ref, rows_ref, out_ref, a1_ref, a2_ref, *, chunk):
    cells = cell_ref.shape[1]
    high = cells // 256
    for h in range(high):
        part = cell_ref[:, h * 256 : (h + 1) * 256]
        top = part.astype(BF16)
        a1_ref[h * 16 : (h + 1) * 16, :] = top
        a2_ref[h * 16 : (h + 1) * 16, :] = (part - top.astype(F32)).astype(BF16)
    tiles = out_ref.shape[0]

    for step in range(tiles // chunk):
        width = chunk * LANES
        base = step * chunk
        cell = jnp.concatenate([index_ref[base + t] for t in range(chunk)], axis=1)
        hi = lax.shift_right_logical(cell, 8)
        lo = cell & 255
        level = lax.broadcasted_iota(jnp.int32, (256, width), 0)
        pick = jnp.where(level == lo, 1.0, 0.0).astype(BF16)
        found = jnp.dot(a1_ref[...], pick, preferred_element_type=F32) + jnp.dot(
            a2_ref[...], pick, preferred_element_type=F32
        )
        hi = jnp.broadcast_to(hi, (16, width))
        total = jnp.zeros((16, width), F32)
        for h in range(high):
            total = jnp.where(hi == h, found[h * 16 : (h + 1) * 16, :], total)
        for t in range(chunk):
            out_ref[base + t] = total[:, t * LANES : (t + 1) * LANES] * rows_ref[base + t, 6:7, :]


def pack_rows(ends_ref, came_ref, packed_ref):
    sources, channels, _ = came_ref.shape
    lane = lax.broadcasted_iota(jnp.int32, (channels, LANES), 1)

    def body(s, carry):
        offset = ends_ref[0, s]
        base = offset // LANES
        shift = offset % LANES
        tile = pltpu.roll(came_ref[s], shift, 1)
        pltpu.store(packed_ref.at[base], tile, mask=lane >= shift)
        pltpu.store(packed_ref.at[base + 1], tile, mask=lane < shift)
        return carry

    lax.fori_loop(0, sources, body, 0, unroll=32)
    return jnp.concatenate([packed_ref[b] for b in range(packed_ref.shape[0] - 1)], axis=1)


def half_angle(turns):
    r = turns - jnp.round(turns)
    u = r * r
    v = u - SIN_A
    half_sin = (v * v + SIN_B) * r
    w = u - COS_A
    half_cos = w * w - COS_B
    return (half_sin * half_sin).astype(BF16), (half_sin * half_cos).astype(BF16)


def masked_parts(parts_ref, f):
    parts = parts_ref[...]
    level = lax.broadcasted_iota(jnp.int32, parts.shape, 0)
    return jnp.where((level >= 32 * f) & (level < 32 * f + 32), parts.astype(F32), 0.0).astype(BF16)


def phase_kernel(ends_ref, wave_ref, came_ref, parts_ref, t_ref, s_ref, rows_ref, y_ref, packed_ref):
    live_own = rows_ref.shape[1]

    @pl.when(pl.program_id(0) == 0)
    def _():
        rows = pack_rows(ends_ref, came_ref, packed_ref)
        rows_ref[...] = rows
        turned = []
        for f in range(FREQS):
            y1, y2, y3 = bf16_parts(rows[0:3] * (wave_ref[f] * (0.5 / math.pi)))
            turned += [y1, y2, y3, y1, y2, y1, y3, y2, jnp.zeros((8, live_own), F32)]
        y_ref[...] = jnp.concatenate(turned, axis=0).T.astype(BF16)

    for f in range(FREQS):
        parts = masked_parts(parts_ref, f)
        for i in range(live_own // PIECE):
            at = slice(i * PIECE, (i + 1) * PIECE)
            turns = jnp.dot(y_ref[at, :], parts, preferred_element_type=F32)
            t_ref[0, f, at, :], s_ref[0, f, at, :] = half_angle(turns)


def radiate_kernel(
    ends_ref, wave_ref, came_ref, rows_ref, y_ref, parts_ref, basis_ref, first_t_ref, first_s_ref,
    t_ref, s_ref, far_ref, packed_ref, src_ref, t_sem, s_sem,
):
    live_own = rows_ref.shape[1]
    step = pl.program_id(0)
    steps = pl.num_programs(0)
    half, _, _, width = first_t_ref.shape

    def fetch(i):
        return (
            pltpu.make_async_copy(first_t_ref.at[i], t_ref.at[i], t_sem.at[i]),
            pltpu.make_async_copy(first_s_ref.at[i], s_ref.at[i], s_sem.at[i]),
        )

    @pl.when(step == 0)
    def _():
        for i in range(half):
            for copy in fetch(i):
                copy.start()
        rows = pack_rows(ends_ref, came_ref, packed_ref)
        normal = rows_ref[3:6]
        for f in range(FREQS):
            real = jnp.concatenate([rows[8 + f : 9 + f], normal * rows[f : f + 1]], axis=0)
            imag = jnp.concatenate([rows[12 + f : 13 + f], normal * rows[4 + f : 5 + f]], axis=0)
            src_ref[f, 0] = jnp.concatenate([real, imag], axis=0).astype(BF16)
            src_ref[f, 1] = jnp.concatenate([imag, -real], axis=0).astype(BF16)

    def project(f, total_t, total_s, basis):
        whole = jnp.sum(src_ref[f, 0].astype(F32), axis=1, keepdims=True)
        q = whole - COS_SCALE * total_t + SIN_SCALE * total_s
        weighted = q * jnp.concatenate([basis] * 2, axis=0)
        real_z = jnp.sum(weighted[0:4], axis=0, keepdims=True)
        imag_z = jnp.sum(weighted[4:8], axis=0, keepdims=True)
        return [imag_z * (-wave_ref[f]), real_z * wave_ref[f]]

    first, second = (pl.ds(pl.multiple_of(i * width, width), width) for i in (step, steps + step))
    basis1 = basis_ref[0:4, first]
    basis2 = basis_ref[0:4, second]
    far1, far2 = [], []
    for f in range(FREQS):
        parts = masked_parts(parts_ref, f)
        for i in range(live_own // PIECE):
            at = slice(i * PIECE, (i + 1) * PIECE)
            turns = jnp.dot(y_ref[at, :], parts, preferred_element_type=F32)
            t_ref[steps + step, f, at, :], s_ref[steps + step, f, at, :] = half_angle(turns)
        total_t = jnp.dot(src_ref[f, 0], t_ref[steps + step, f], preferred_element_type=F32)
        total_s = jnp.dot(src_ref[f, 1], s_ref[steps + step, f], preferred_element_type=F32)
        far2 += project(f, total_t, total_s, basis2)
    for copy in fetch(step):
        copy.wait()
    for f in range(FREQS):
        total_t = jnp.dot(src_ref[f, 0], t_ref[step, f], preferred_element_type=F32)
        total_s = jnp.dot(src_ref[f, 1], s_ref[step, f], preferred_element_type=F32)
        far1 += project(f, total_t, total_s, basis1)
    far_ref[:, first] = jnp.concatenate(far1, axis=0)
    far_ref[:, second] = jnp.concatenate(far2, axis=0)


def adjoint_kernel(
    ends_ref, wave_ref, target_ref, weight_ref, basis_ref, rows_ref, t_ref, s_ref, *rest
):
    far_terms, (_t, _s, out_ref, cost_ref, far_ref, flat_ref) = rest[:-6], rest[-6:]
    far = far_terms[0][...]
    if len(far_terms) == 2:
        far = far + far_terms[1][...]
    else:
        far = (far + far_terms[1][...]) + (far_terms[2][...] + far_terms[3][...])
    for f in range(FREQS):
        far_ref[f] = far[2 * f : 2 * f + 2]

    live_own = rows_ref.shape[1]
    blocks = live_own // LANES
    count_dirs = far.shape[1]
    width = t_ref.shape[3]
    mismatch = far - jnp.concatenate([target_ref[f] for f in range(FREQS)], axis=0)
    pull = weight_ref[...] * mismatch
    cost_ref[0] = jnp.sum(pull * mismatch) / count_dirs
    gradient = pull * (2.0 / count_dirs)
    basis = jnp.concatenate([basis_ref[0:4, :]] * 2, axis=0)
    contract = (((1,), (1,)), ((), ()))
    normal = rows_ref[3:6]
    pressure_real, pressure_imag, velocity_real, velocity_imag = [], [], [], []
    for f in range(FREQS):
        real_gz = jnp.broadcast_to(gradient[2 * f + 1 : 2 * f + 2] * wave_ref[f], (4, count_dirs))
        imag_gz = jnp.broadcast_to(gradient[2 * f : 2 * f + 1] * (-wave_ref[f]), (4, count_dirs))
        for_cos = (basis * jnp.concatenate([real_gz, imag_gz], axis=0)).astype(BF16)
        for_sin = (basis * jnp.concatenate([-imag_gz, real_gz], axis=0)).astype(BF16)
        whole = jnp.sum(for_cos.astype(F32), axis=1, keepdims=True)
        total_t = jnp.zeros((8, live_own), F32)
        total_s = jnp.zeros((8, live_own), F32)
        for i in range(t_ref.shape[0]):
            at = slice(i * width, (i + 1) * width)
            total_t += lax.dot_general(for_cos[:, at], t_ref[i, f], contract, preferred_element_type=F32)
            total_s += lax.dot_general(for_sin[:, at], s_ref[i, f], contract, preferred_element_type=F32)
        got = whole - COS_SCALE * total_t + SIN_SCALE * total_s
        pressure_real.append(jnp.sum(normal * got[1:4], axis=0, keepdims=True))
        pressure_imag.append(jnp.sum(normal * got[5:8], axis=0, keepdims=True))
        velocity_real.append(got[0:1])
        velocity_imag.append(got[4:5])
    flat = jnp.concatenate(pressure_real + pressure_imag + velocity_real + velocity_imag, axis=0)
    for b in range(blocks):
        flat_ref[b] = flat[:, b * LANES : (b + 1) * LANES]
    flat_ref[blocks] = jnp.zeros((16, LANES), F32)
    lane = lax.broadcasted_iota(jnp.int32, (16, LANES), 1)

    def body(s, carry):
        offset = ends_ref[0, s]
        base = offset // LANES
        shift = offset % LANES
        back = (LANES - shift) % LANES
        joined = jnp.where(lane >= shift, flat_ref[base], flat_ref[base + 1])
        joined = pltpu.roll(joined, back, 1)
        out_ref[s] = jnp.where(lane < ends_ref[1, s], joined, 0.0)
        return carry

    lax.fori_loop(0, out_ref.shape[0], body, 0, unroll=32)


def scatter_kernel(value_ref, index_ref, out_ref, *, chunk):
    tiles = value_ref.shape[0]
    high = out_ref.shape[1] // 256
    width = chunk * LANES
    contract = (((1,), (1,)), ((), ()))

    def body(step, total):
        base = step * chunk
        cell = jnp.concatenate([index_ref[base + t] for t in range(chunk)], axis=1)
        value = jnp.concatenate([value_ref[base + t] for t in range(chunk)], axis=1)
        hi = lax.shift_right_logical(cell, 8)
        lo = cell & 255
        level = lax.broadcasted_iota(jnp.int32, (256, width), 0)
        pick = jnp.where(level == lo, 1.0, 0.0).astype(BF16)
        value = value.astype(BF16)
        hi = jnp.broadcast_to(hi, (16, width)).astype(F32).astype(BF16)
        zero = jnp.zeros((16, width), BF16)
        spread = jnp.concatenate([jnp.where(hi == float(h), value, zero) for h in range(high)], axis=0)
        return total + lax.dot_general(spread, pick, contract, preferred_element_type=F32)

    total = jnp.zeros((high * 16, 256), F32)
    for step in range(tiles // chunk):
        total = body(step, total)
    for h in range(high):
        out_ref[:, h * 256 : (h + 1) * 256] = total[h * 16 : (h + 1) * 16, :]


def smem():
    return pl.BlockSpec(memory_space=pltpu.SMEM)


def params():
    return pltpu.CompilerParams(vmem_limit_bytes=VMEM_BYTES)


def to_tiles(x, cap):
    owners, channels, _ = x.shape
    if cap == LANES:
        return x
    many = LANES // cap
    x = x.reshape(owners // many, many, channels, cap).transpose(0, 2, 1, 3)
    return x.reshape(owners // many, channels, LANES)


def from_tiles(x, cap):
    tiles, channels, _ = x.shape
    if cap == LANES:
        return x
    many = LANES // cap
    x = x.reshape(tiles, channels, many, cap).transpose(0, 2, 1, 3)
    return x.reshape(tiles * many, channels, cap)


def all_sum(x):
    gx, gy = (lax.axis_size(axis) for axis in AXES)
    low = gy.bit_length() - 1
    rest = [b for b in range((gx * gy).bit_length() - 1) if b != low]
    rounds = [[low]]
    if low % 2:
        rounds.append([rest.pop(0), rest.pop(-1)])
    rounds += [rest[i : i + 2] for i in range(0, len(rest), 2)]
    for bits in rounds:
        masks = [sum(1 << b for k, b in enumerate(bits) if code >> k & 1) for code in range(1, 1 << len(bits))]
        came = [lax.ppermute(x, AXES, [(i, i ^ m) for i in range(gx * gy)]) for m in masks]
        if bits is rounds[-1]:
            return [x] + came
        x = x + came[0] if len(came) == 1 else (x + came[0]) + (came[1] + came[2])


def on_device(cell_state, geometry, surface_cell, counts, wavenumbers, target, direction_weight):
    owners = lax.axis_size(AXES)
    rows_dev = surface_cell.shape[0]
    cells = cell_state.shape[1]
    cap = rows_dev // owners
    live_own = rows_dev // 4
    count_dirs = target.shape[2]
    tiles = rows_dev // LANES
    high = cells // 256
    basis, parts = direction_tables(count_dirs)
    basis, parts, wavenumbers, cell_state = (
        pltpu.with_memory_space_constraint(x, pltpu.HBM)
        for x in (jnp.asarray(basis), jnp.asarray(parts), wavenumbers, cell_state)
    )
    vmem = pl.BlockSpec(memory_space=pltpu.VMEM)

    share = (counts // owners).astype(F32)
    rows = jnp.concatenate([geometry, jnp.broadcast_to(share[None, :], (1, rows_dev))], axis=0)
    rows = rows.reshape(8, cap, owners).transpose(2, 0, 1)
    came = lax.all_to_all(rows, AXES, split_axis=0, concat_axis=0, tiled=True)
    index = to_tiles(surface_cell.reshape(cap, owners).T.reshape(owners, 1, cap), cap)
    outgoing = pl.pallas_call(
        functools.partial(gather_kernel, chunk=4),
        in_specs=[vmem, vmem, vmem],
        out_shape=jax.ShapeDtypeStruct((tiles, 16, LANES), F32),
        scratch_shapes=[pltpu.VMEM((high * 16, 256), BF16), pltpu.VMEM((high * 16, 256), BF16)],
        compiler_params=params(),
        name="gather_rows",
    )(cell_state, index, to_tiles(rows, cap))
    values = lax.all_to_all(from_tiles(outgoing, cap), AXES, split_axis=0, concat_axis=0, tiled=True)
    me, other = jnp.arange(2 * owners)[:, None], jnp.arange(owners)[None, :]
    counted = jnp.where(me < owners, other < me, other == me - owners)
    ends = jnp.sum(jnp.where(counted, came[:, 7, 0][None, :], 0.0), axis=1).astype(jnp.int32).reshape(2, owners)
    if cap < LANES:
        came = jnp.pad(came, ((0, 0), (0, 0), (0, LANES - cap)))
        values = jnp.pad(values, ((0, 0), (0, 0), (0, LANES - cap)))

    width = 256
    half = count_dirs // width // 2
    packs = live_own // LANES + 1
    first = pltpu.HBM((half, FREQS, live_own, width), BF16)
    held = pltpu.VMEM((2 * half, FREQS, live_own, width), BF16)
    block = pl.BlockSpec((1, FREQS, live_own, width), lambda i: (i, 0, 0, 0))
    first_t, first_s, kept, turned = pl.pallas_call(
        phase_kernel,
        grid=(half,),
        in_specs=[smem(), smem(), vmem, pl.BlockSpec((32 * FREQS, width), lambda i: (0, i))],
        out_specs=[block, block, vmem, vmem],
        out_shape=[
            first, first,
            pltpu.HBM((8, live_own), F32),
            pltpu.HBM((live_own, 32 * FREQS), BF16),
        ],
        scratch_shapes=[pltpu.VMEM((packs, 8, LANES), F32)],
        compiler_params=params(),
        name="phases",
    )(ends, wavenumbers, came, parts)

    hbm = pl.BlockSpec(memory_space=pltpu.HBM)
    t_all, s_all, far = pl.pallas_call(
        radiate_kernel,
        grid=(half,),
        in_specs=[
            smem(), smem(), vmem, vmem, vmem,
            pl.BlockSpec((32 * FREQS, width), lambda i: (0, half + i)),
            vmem, hbm, hbm,
        ],
        out_specs=[vmem] * 3,
        out_shape=[held, held, pltpu.VMEM((2 * FREQS, count_dirs), F32)],
        scratch_shapes=[
            pltpu.VMEM((packs, 16, LANES), F32),
            pltpu.VMEM((FREQS, 2, 8, live_own), BF16),
            pltpu.SemaphoreType.DMA((half,)),
            pltpu.SemaphoreType.DMA((half,)),
        ],
        compiler_params=params(),
        name="radiate",
    )(ends, wavenumbers, values, kept, turned, parts, basis, first_t, first_s)

    far_terms = [pltpu.with_memory_space_constraint(x, pltpu.VMEM) for x in all_sum(far)]

    _, _, back, objective, far = pl.pallas_call(
        adjoint_kernel,
        in_specs=[smem(), smem()] + [vmem] * (6 + len(far_terms)),
        out_specs=[vmem, vmem, vmem, smem(), vmem],
        out_shape=[
            held, held,
            jax.ShapeDtypeStruct((owners, 16, LANES), F32),
            jax.ShapeDtypeStruct((1,), F32),
            jax.ShapeDtypeStruct(target.shape, F32),
        ],
        input_output_aliases={6: 0, 7: 1},
        scratch_shapes=[pltpu.VMEM((packs, 16, LANES), F32)],
        compiler_params=params(),
        name="adjoint",
    )(
        ends, wavenumbers, target, direction_weight.reshape(1, count_dirs), basis, kept, t_all, s_all, *far_terms,
    )
    returned = lax.all_to_all(back[:, :, :cap], AXES, split_axis=0, concat_axis=0, tiled=True)
    cell_adjoint = pl.pallas_call(
        functools.partial(scatter_kernel, chunk=4),
        in_specs=[vmem, vmem],
        out_shape=jax.ShapeDtypeStruct(cell_state.shape, F32),
        compiler_params=params(),
        name="scatter_rows",
    )(to_tiles(returned, cap), index)
    return (far, objective[0], cell_adjoint)


def solution(mesh):
    placed = (
        P(None, AXES),
        P(None, AXES),
        P(AXES),
        P(AXES),
        P(),
        P(),
        P(),
    )
    return jax.shard_map(
        on_device,
        mesh=mesh,
        in_specs=placed,
        out_specs=(P(), P(), P(None, AXES)),
        check_vma=False,
    )
```

```python
import functools
import math

import jax
import jax.numpy as jnp
import numpy as np
from jax import lax
from jax.experimental import pallas as pl
from jax.experimental.pallas import tpu as pltpu
from jax.sharding import PartitionSpec as P

GOLDEN = math.pi * (3.0 - math.sqrt(5.0))
AXES = ("gx", "gy")
F32 = jnp.float32
BF16 = jnp.bfloat16
LANES = 128
FREQS = 4
VMEM_BYTES = 24 * 2**20
PIECE = 1024

SIN_K, SIN_A, SIN_B = 2.299546, 1.116939, 0.118212
COS_K, COS_A, COS_B = 3.583841, 0.682394, 0.186797
COS_SCALE = 2.0 * SIN_K * SIN_K
SIN_SCALE = 2.0 * SIN_K * COS_K


def direction_tables(count_dirs):
    lattice = np.arange(count_dirs).astype(np.float32)
    height = (np.float32(1.0) - (np.float32(2.0) * lattice + np.float32(1.0)) / np.float32(count_dirs)).astype(np.float32)
    radius_xy = np.sqrt(np.float32(1.0) - height * height).astype(np.float32)
    azimuth = np.mod(lattice * np.float32(GOLDEN), np.float32(2.0 * math.pi)).astype(np.float32)
    d = np.stack([radius_xy * np.cos(azimuth), radius_xy * np.sin(azimuth), height]).astype(np.float32)
    basis = np.concatenate([np.ones((1, count_dirs), np.float32), d, np.zeros((4, count_dirs), np.float32)])
    d1 = d.astype(jnp.bfloat16)
    d2 = (d - d1.astype(np.float32)).astype(jnp.bfloat16)
    d3 = (d - d1.astype(np.float32) - d2.astype(np.float32)).astype(jnp.bfloat16)
    parts = np.concatenate([d1, d1, d1, d2, d2, d3, d2, d3, np.zeros((8, count_dirs), d1.dtype)])
    return basis, np.concatenate([parts] * FREQS)


def bf16_parts(x):
    x1 = x.astype(BF16).astype(F32)
    x2 = (x - x1).astype(BF16).astype(F32)
    return x1, x2, x - x1 - x2


def gather_kernel(cell_ref, index_ref, rows_ref, out_ref, a1_ref, a2_ref, *, chunk):
    cells = cell_ref.shape[1]
    high = cells // 256
    for h in range(high):
        part = cell_ref[:, h * 256 : (h + 1) * 256]
        top = part.astype(BF16)
        a1_ref[h * 16 : (h + 1) * 16, :] = top
        a2_ref[h * 16 : (h + 1) * 16, :] = (part - top.astype(F32)).astype(BF16)
    tiles = out_ref.shape[0]

    for step in range(tiles // chunk):
        width = chunk * LANES
        base = step * chunk
        cell = jnp.concatenate([index_ref[base + t] for t in range(chunk)], axis=1)
        hi = lax.shift_right_logical(cell, 8)
        lo = cell & 255
        level = lax.broadcasted_iota(jnp.int32, (256, width), 0)
        pick = jnp.where(level == lo, 1.0, 0.0).astype(BF16)
        found = jnp.dot(a1_ref[...], pick, preferred_element_type=F32) + jnp.dot(
            a2_ref[...], pick, preferred_element_type=F32
        )
        hi = jnp.broadcast_to(hi, (16, width))
        total = jnp.zeros((16, width), F32)
        for h in range(high):
            total = jnp.where(hi == h, found[h * 16 : (h + 1) * 16, :], total)
        for t in range(chunk):
            out_ref[base + t] = total[:, t * LANES : (t + 1) * LANES] * rows_ref[base + t, 6:7, :]


def pack_rows(ends_ref, came_ref, packed_ref):
    sources, channels, _ = came_ref.shape
    lane = lax.broadcasted_iota(jnp.int32, (channels, LANES), 1)

    def body(s, carry):
        offset = ends_ref[0, s]
        base = offset // LANES
        shift = offset % LANES
        tile = pltpu.roll(came_ref[s], shift, 1)
        pltpu.store(packed_ref.at[base], tile, mask=lane >= shift)
        pltpu.store(packed_ref.at[base + 1], tile, mask=lane < shift)
        return carry

    lax.fori_loop(0, sources, body, 0, unroll=32)
    return jnp.concatenate([packed_ref[b] for b in range(packed_ref.shape[0] - 1)], axis=1)


def half_angle(turns):
    r = turns - jnp.round(turns)
    u = r * r
    v = u - SIN_A
    half_sin = (v * v + SIN_B) * r
    w = u - COS_A
    half_cos = w * w - COS_B
    return (half_sin * half_sin).astype(BF16), (half_sin * half_cos).astype(BF16)


def masked_parts(parts, f):
    level = lax.broadcasted_iota(jnp.int32, parts.shape, 0)
    return jnp.where((level >= 32 * f) & (level < 32 * f + 32), parts.astype(F32), 0.0).astype(BF16)


def phase_kernel(ends_ref, wave_ref, came_ref, parts_ref, t_ref, s_ref, rows_ref, y_ref, packed_ref):
    live_own = rows_ref.shape[1]

    @pl.when(pl.program_id(0) == 0)
    def _():
        rows = pack_rows(ends_ref, came_ref, packed_ref)
        rows_ref[...] = rows
        turned = []
        for f in range(FREQS):
            y1, y2, y3 = bf16_parts(rows[0:3] * (wave_ref[f] * (0.5 / math.pi)))
            turned += [y1, y2, y3, y1, y2, y1, y3, y2, jnp.zeros((8, live_own), F32)]
        y_ref[...] = jnp.concatenate(turned, axis=0).T.astype(BF16)

    for f in range(FREQS):
        parts = masked_parts(parts_ref[...], f)
        for i in range(live_own // PIECE):
            at = slice(i * PIECE, (i + 1) * PIECE)
            turns = jnp.dot(y_ref[at, :], parts, preferred_element_type=F32)
            t_ref[0, f, at, :], s_ref[0, f, at, :] = half_angle(turns)


def radiate_kernel(
    ends_ref, wave_ref, came_ref, rows_ref, y_ref, parts_ref, basis_ref, first_t_ref, first_s_ref,
    t_ref, s_ref, far_ref, packed_ref, src_ref, t_sem, s_sem, *, half_steps,
):
    live_own = rows_ref.shape[1]
    step = pl.program_id(0)
    steps = half_steps
    half, _, _, width = first_t_ref.shape

    def fetch(i):
        return (
            pltpu.make_async_copy(first_t_ref.at[i], t_ref.at[i], t_sem.at[i]),
            pltpu.make_async_copy(first_s_ref.at[i], s_ref.at[i], s_sem.at[i]),
        )

    @pl.when(step == 0)
    def _():
        for i in range(half):
            for copy in fetch(i):
                copy.start()
        rows = pack_rows(ends_ref, came_ref, packed_ref)
        normal = rows_ref[3:6]
        for f in range(FREQS):
            real = jnp.concatenate([rows[8 + f : 9 + f], normal * rows[f : f + 1]], axis=0)
            imag = jnp.concatenate([rows[12 + f : 13 + f], normal * rows[4 + f : 5 + f]], axis=0)
            src_ref[f, 0] = jnp.concatenate([real, imag], axis=0).astype(BF16)
            src_ref[f, 1] = jnp.concatenate([imag, -real], axis=0).astype(BF16)

    def project(f, total_t, total_s, basis):
        whole = jnp.sum(src_ref[f, 0].astype(F32), axis=1, keepdims=True)
        q = whole - COS_SCALE * total_t + SIN_SCALE * total_s
        weighted = q * jnp.concatenate([basis] * 2, axis=0)
        real_z = jnp.sum(weighted[0:4], axis=0, keepdims=True)
        imag_z = jnp.sum(weighted[4:8], axis=0, keepdims=True)
        return [imag_z * (-wave_ref[f]), real_z * wave_ref[f]]

    per = half // steps
    for j in range(per):
        tile = step * per + j
        at = pl.ds(pl.multiple_of((half + tile) * width, width), width)
        basis = basis_ref[0:4, at]
        far = []
        for f in range(FREQS):
            parts = masked_parts(parts_ref[:, j * width : (j + 1) * width], f)
            turns = jnp.dot(y_ref[...], parts, preferred_element_type=F32)
            t_ref[half + tile, f], s_ref[half + tile, f] = half_angle(turns)
            total_t = jnp.dot(src_ref[f, 0], t_ref[half + tile, f], preferred_element_type=F32)
            total_s = jnp.dot(src_ref[f, 1], s_ref[half + tile, f], preferred_element_type=F32)
            far += project(f, total_t, total_s, basis)
        far_ref[:, at] = jnp.concatenate(far, axis=0)
    for j in range(per):
        tile = step * per + j
        for copy in fetch(tile):
            copy.wait()
    for j in range(per):
        tile = step * per + j
        at = pl.ds(pl.multiple_of(tile * width, width), width)
        basis = basis_ref[0:4, at]
        far = []
        for f in range(FREQS):
            total_t = jnp.dot(src_ref[f, 0], t_ref[tile, f], preferred_element_type=F32)
            total_s = jnp.dot(src_ref[f, 1], s_ref[tile, f], preferred_element_type=F32)
            far += project(f, total_t, total_s, basis)
        far_ref[:, at] = jnp.concatenate(far, axis=0)


def adjoint_kernel(
    ends_ref, wave_ref, target_ref, weight_ref, basis_ref, rows_ref, t_ref, s_ref, *rest
):
    far_terms, (_t, _s, out_ref, cost_ref, far_ref, flat_ref) = rest[:-6], rest[-6:]
    far = far_terms[0][...]
    if len(far_terms) == 2:
        far = far + far_terms[1][...]
    else:
        far = (far + far_terms[1][...]) + (far_terms[2][...] + far_terms[3][...])
    for f in range(FREQS):
        far_ref[f] = far[2 * f : 2 * f + 2]

    live_own = rows_ref.shape[1]
    blocks = live_own // LANES
    count_dirs = far.shape[1]
    width = t_ref.shape[3]
    mismatch = far - jnp.concatenate([target_ref[f] for f in range(FREQS)], axis=0)
    pull = weight_ref[...] * mismatch
    cost_ref[0] = jnp.sum(pull * mismatch) / count_dirs
    gradient = pull * (2.0 / count_dirs)
    basis = jnp.concatenate([basis_ref[0:4, :]] * 2, axis=0)
    contract = (((1,), (1,)), ((), ()))
    normal = rows_ref[3:6]
    pressure_real, pressure_imag, velocity_real, velocity_imag = [], [], [], []
    for f in range(FREQS):
        real_gz = jnp.broadcast_to(gradient[2 * f + 1 : 2 * f + 2] * wave_ref[f], (4, count_dirs))
        imag_gz = jnp.broadcast_to(gradient[2 * f : 2 * f + 1] * (-wave_ref[f]), (4, count_dirs))
        for_cos = (basis * jnp.concatenate([real_gz, imag_gz], axis=0)).astype(BF16)
        for_sin = (basis * jnp.concatenate([-imag_gz, real_gz], axis=0)).astype(BF16)
        whole = jnp.sum(for_cos.astype(F32), axis=1, keepdims=True)
        total_t = jnp.zeros((8, live_own), F32)
        total_s = jnp.zeros((8, live_own), F32)
        for i in range(t_ref.shape[0]):
            at = slice(i * width, (i + 1) * width)
            total_t += lax.dot_general(for_cos[:, at], t_ref[i, f], contract, preferred_element_type=F32)
            total_s += lax.dot_general(for_sin[:, at], s_ref[i, f], contract, preferred_element_type=F32)
        got = whole - COS_SCALE * total_t + SIN_SCALE * total_s
        pressure_real.append(jnp.sum(normal * got[1:4], axis=0, keepdims=True))
        pressure_imag.append(jnp.sum(normal * got[5:8], axis=0, keepdims=True))
        velocity_real.append(got[0:1])
        velocity_imag.append(got[4:5])
    flat = jnp.concatenate(pressure_real + pressure_imag + velocity_real + velocity_imag, axis=0)
    for b in range(blocks):
        flat_ref[b] = flat[:, b * LANES : (b + 1) * LANES]
    flat_ref[blocks] = jnp.zeros((16, LANES), F32)
    lane = lax.broadcasted_iota(jnp.int32, (16, LANES), 1)

    def body(s, carry):
        offset = ends_ref[0, s]
        base = offset // LANES
        shift = offset % LANES
        back = (LANES - shift) % LANES
        joined = jnp.where(lane >= shift, flat_ref[base], flat_ref[base + 1])
        joined = pltpu.roll(joined, back, 1)
        out_ref[s] = jnp.where(lane < ends_ref[1, s], joined, 0.0)
        return carry

    lax.fori_loop(0, out_ref.shape[0], body, 0, unroll=32)


def scatter_kernel(value_ref, index_ref, out_ref, *, chunk):
    tiles = value_ref.shape[0]
    high = out_ref.shape[1] // 256
    width = chunk * LANES
    contract = (((1,), (1,)), ((), ()))

    def body(step, total):
        base = step * chunk
        cell = jnp.concatenate([index_ref[base + t] for t in range(chunk)], axis=1)
        value = jnp.concatenate([value_ref[base + t] for t in range(chunk)], axis=1)
        hi = lax.shift_right_logical(cell, 8)
        lo = cell & 255
        level = lax.broadcasted_iota(jnp.int32, (256, width), 0)
        pick = jnp.where(level == lo, 1.0, 0.0).astype(BF16)
        value = value.astype(BF16)
        hi = jnp.broadcast_to(hi, (16, width)).astype(F32).astype(BF16)
        zero = jnp.zeros((16, width), BF16)
        spread = jnp.concatenate([jnp.where(hi == float(h), value, zero) for h in range(high)], axis=0)
        return total + lax.dot_general(spread, pick, contract, preferred_element_type=F32)

    total = jnp.zeros((high * 16, 256), F32)
    for step in range(tiles // chunk):
        total = body(step, total)
    for h in range(high):
        out_ref[:, h * 256 : (h + 1) * 256] = total[h * 16 : (h + 1) * 16, :]


def smem():
    return pl.BlockSpec(memory_space=pltpu.SMEM)


def params():
    return pltpu.CompilerParams(vmem_limit_bytes=VMEM_BYTES)


def to_tiles(x, cap):
    owners, channels, _ = x.shape
    if cap == LANES:
        return x
    many = LANES // cap
    x = x.reshape(owners // many, many, channels, cap).transpose(0, 2, 1, 3)
    return x.reshape(owners // many, channels, LANES)


def from_tiles(x, cap):
    tiles, channels, _ = x.shape
    if cap == LANES:
        return x
    many = LANES // cap
    x = x.reshape(tiles, channels, many, cap).transpose(0, 2, 1, 3)
    return x.reshape(tiles * many, channels, cap)


def all_sum(x):
    gx, gy = (lax.axis_size(axis) for axis in AXES)
    low = gy.bit_length() - 1
    rest = [b for b in range((gx * gy).bit_length() - 1) if b != low]
    rounds = [[low]]
    if low % 2:
        rounds.append([rest.pop(0), rest.pop(-1)])
    rounds += [rest[i : i + 2] for i in range(0, len(rest), 2)]
    for bits in rounds:
        masks = [sum(1 << b for k, b in enumerate(bits) if code >> k & 1) for code in range(1, 1 << len(bits))]
        came = [lax.ppermute(x, AXES, [(i, i ^ m) for i in range(gx * gy)]) for m in masks]
        if bits is rounds[-1]:
            return [x] + came
        x = x + came[0] if len(came) == 1 else (x + came[0]) + (came[1] + came[2])


def on_device(cell_state, geometry, surface_cell, counts, wavenumbers, target, direction_weight):
    owners = lax.axis_size(AXES)
    rows_dev = surface_cell.shape[0]
    cells = cell_state.shape[1]
    cap = rows_dev // owners
    live_own = rows_dev // 4
    count_dirs = target.shape[2]
    tiles = rows_dev // LANES
    high = cells // 256
    basis, parts = direction_tables(count_dirs)
    basis, parts, wavenumbers, cell_state = (
        pltpu.with_memory_space_constraint(x, pltpu.HBM)
        for x in (jnp.asarray(basis), jnp.asarray(parts), wavenumbers, cell_state)
    )
    vmem = pl.BlockSpec(memory_space=pltpu.VMEM)

    share = (counts // owners).astype(F32)
    rows = jnp.concatenate([geometry, jnp.broadcast_to(share[None, :], (1, rows_dev))], axis=0)
    rows = rows.reshape(8, cap, owners).transpose(2, 0, 1)
    came = lax.all_to_all(rows, AXES, split_axis=0, concat_axis=0, tiled=True)
    index = to_tiles(surface_cell.reshape(cap, owners).T.reshape(owners, 1, cap), cap)
    outgoing = pl.pallas_call(
        functools.partial(gather_kernel, chunk=4),
        in_specs=[vmem, vmem, vmem],
        out_shape=jax.ShapeDtypeStruct((tiles, 16, LANES), F32),
        scratch_shapes=[pltpu.VMEM((high * 16, 256), BF16), pltpu.VMEM((high * 16, 256), BF16)],
        compiler_params=params(),
        name="gather_rows",
    )(cell_state, index, to_tiles(rows, cap))
    values = lax.all_to_all(from_tiles(outgoing, cap), AXES, split_axis=0, concat_axis=0, tiled=True)
    me, other = jnp.arange(2 * owners)[:, None], jnp.arange(owners)[None, :]
    counted = jnp.where(me < owners, other < me, other == me - owners)
    ends = jnp.sum(jnp.where(counted, came[:, 7, 0][None, :], 0.0), axis=1).astype(jnp.int32).reshape(2, owners)
    if cap < LANES:
        came = jnp.pad(came, ((0, 0), (0, 0), (0, LANES - cap)))
        values = jnp.pad(values, ((0, 0), (0, 0), (0, LANES - cap)))

    width = 256
    half = count_dirs // width // 2
    packs = live_own // LANES + 1
    first = pltpu.HBM((half, FREQS, live_own, width), BF16)
    held = pltpu.VMEM((2 * half, FREQS, live_own, width), BF16)
    block = pl.BlockSpec((1, FREQS, live_own, width), lambda i: (i, 0, 0, 0))
    first_t, first_s, kept, turned = pl.pallas_call(
        phase_kernel,
        grid=(half,),
        in_specs=[smem(), smem(), vmem, pl.BlockSpec((32 * FREQS, width), lambda i: (0, i))],
        out_specs=[block, block, vmem, vmem],
        out_shape=[
            first, first,
            pltpu.HBM((8, live_own), F32),
            pltpu.HBM((live_own, 32 * FREQS), BF16),
        ],
        scratch_shapes=[pltpu.VMEM((packs, 8, LANES), F32)],
        compiler_params=params(),
        name="phases",
    )(ends, wavenumbers, came, parts)

    hbm = pl.BlockSpec(memory_space=pltpu.HBM)
    t_all, s_all, far = pl.pallas_call(
        functools.partial(radiate_kernel, half_steps=half // 4),
        grid=(half // 4,),
        in_specs=[
            smem(), smem(), vmem, vmem, vmem,
            pl.BlockSpec((32 * FREQS, 4 * width), lambda i: (0, half // 4 + i)),
            vmem, hbm, hbm,
        ],
        out_specs=[vmem] * 3,
        out_shape=[held, held, pltpu.VMEM((2 * FREQS, count_dirs), F32)],
        scratch_shapes=[
            pltpu.VMEM((packs, 16, LANES), F32),
            pltpu.VMEM((FREQS, 2, 8, live_own), BF16),
            pltpu.SemaphoreType.DMA((half,)),
            pltpu.SemaphoreType.DMA((half,)),
        ],
        compiler_params=params(),
        name="radiate",
    )(ends, wavenumbers, values, kept, turned, parts, basis, first_t, first_s)

    far_terms = [pltpu.with_memory_space_constraint(x, pltpu.VMEM) for x in all_sum(far)]

    _, _, back, objective, far = pl.pallas_call(
        adjoint_kernel,
        in_specs=[smem(), smem()] + [vmem] * (6 + len(far_terms)),
        out_specs=[vmem, vmem, vmem, smem(), vmem],
        out_shape=[
            held, held,
            jax.ShapeDtypeStruct((owners, 16, LANES), F32),
            jax.ShapeDtypeStruct((1,), F32),
            jax.ShapeDtypeStruct(target.shape, F32),
        ],
        input_output_aliases={6: 0, 7: 1},
        scratch_shapes=[pltpu.VMEM((packs, 16, LANES), F32)],
        compiler_params=params(),
        name="adjoint",
    )(
        ends, wavenumbers, target, direction_weight.reshape(1, count_dirs), basis, kept, t_all, s_all, *far_terms,
    )
    returned = lax.all_to_all(back[:, :, :cap], AXES, split_axis=0, concat_axis=0, tiled=True)
    cell_adjoint = pl.pallas_call(
        functools.partial(scatter_kernel, chunk=4),
        in_specs=[vmem, vmem],
        out_shape=jax.ShapeDtypeStruct(cell_state.shape, F32),
        compiler_params=params(),
        name="scatter_rows",
    )(to_tiles(returned, cap), index)
    return (far, objective[0], cell_adjoint)


def solution(mesh):
    placed = (
        P(None, AXES),
        P(None, AXES),
        P(AXES),
        P(AXES),
        P(),
        P(),
        P(),
    )
    return jax.shard_map(
        on_device,
        mesh=mesh,
        in_specs=placed,
        out_specs=(P(), P(), P(None, AXES)),
        check_vma=False,
    )
```
